32 devices in a mesh: dp: 16 (over z, y, core), chan: 2 (over x).
Axes of the slice: x: 2, y: 2, z: 4, core: 2. Of those that a mesh axis runs over, the one named last changes fastest.
Arguments:
- h_in: bfloat16 [16, 1280, 1024], P('dp', 'chan'), may hold values from -40 to 40
- skip: bfloat16 [16, 1280, 1024], P('dp', 'chan'), may hold values from -6 to 6
- emb: bfloat16 [16, 1280], P('dp'), may hold values from -6 to 6
- w_emb: bfloat16 [1280, 1280], P('dp', 'chan'), may hold values from -0.15625 to 0.15625
- b_emb: float32 [1280], P('chan'), may hold values from -3 to 3
- gn_gain: float32 [1280], P('chan'), may hold values from 0.1 to 1.9
- gn_bias: float32 [1280], P('chan'), may hold values from -3 to 3
- w_conv: bfloat16 [9, 1280, 1280], P(None, 'dp', 'chan'), may hold values from -0.0546875 to 0.0546875
- b_conv: float32 [1280], P('chan'), may hold values from -3 to 3
Outputs:
- block_out: bfloat16 [16, 1280, 1024], P('dp', 'chan')
The draws below stay inside these ranges and needn't reach their ends.
All inputs are finite; a program needn't handle non-finite values.
Results may differ from the reference program's by a relative error of at most 0.0036.
Values may be sent and summed in bfloat16 or wider, within the bound.
No kernel may reach another device: no remote copies, remote signals or barrier semaphores. Data moves between devices by JAX's collectives and lax.ppermute only.
A program may use at most 128 MiB of HBM per device.

```python
import jax
import jax.numpy as jnp
from jax import lax

C = 1280
GROUPS = 32
C_EMB = 1280
HEIGHT = 32
WIDTH = 32
BATCH = 16
HW = 1024


def draw_h_in(key, part):
    keys = jax.random.split(jax.random.fold_in(key, 17), 3)
    span = jnp.log(10.0)
    channel_scale = jnp.exp(jax.random.uniform(keys[1], (1, C, 1), jnp.float32, 0.0, span))
    place_scale = jnp.exp(jax.random.uniform(keys[2], (1, 1, HEIGHT * WIDTH), jnp.float32, 0.0, span))
    scale = channel_scale * place_scale / 10.0
    base = jax.random.truncated_normal(keys[0], -4.0, 4.0, (BATCH, C, HEIGHT * WIDTH), jnp.float32)
    return (base * scale).astype(jnp.bfloat16)


def levels(rng, dims, pieces, smallest, high):
    level = 1.0
    for dim, blocks in pieces:
        steps = jax.random.uniform(jax.random.fold_in(jax.random.fold_in(rng, 6), dim), (blocks,), jnp.float32, smallest / len(pieces), high / len(pieces))
        level = level * jnp.repeat(jnp.exp(steps), dims[dim] // blocks).reshape((-1,) + (1,) * (len(dims) - 1 - dim))
    return level


def scatter_about(rng, dims, width, bound, cuts=(), dtype=jnp.bfloat16):
    values = width * jax.random.normal(rng, dims, jnp.float32)
    if cuts:
        values = values * levels(rng, dims, cuts, -0.22, 0.18)
    return jnp.clip(values, -bound, bound).astype(dtype)


def setup_inputs(seed: int = 0) -> dict:
    arg_keys = jax.random.split(jax.random.key(seed), 10)
    return {
        "h_in": draw_h_in(jax.random.fold_in(arg_keys[9], 71), 0),
        "skip": scatter_about(arg_keys[1], (BATCH, C, HW), 1.0, 6.0, ((0, 16), (1, 2))),
        "emb": scatter_about(arg_keys[2], (BATCH, C_EMB), 1.0, 6.0, ((0, 16),)),
        "w_emb": scatter_about(arg_keys[3], (C_EMB, C), C_EMB ** -0.5, 0.15625, ((0, 16), (1, 2))),
        "b_emb": scatter_about(arg_keys[4], (C,), 0.5, 3.0, ((0, 2),), jnp.float32),
        "gn_gain": jnp.clip(1.0 + 0.18 * jax.random.normal(arg_keys[5], (C,), jnp.float32), 0.1, 1.9),
        "gn_bias": scatter_about(arg_keys[6], (C,), 0.5, 3.0, ((0, 2),), jnp.float32),
        "w_conv": scatter_about(arg_keys[7], (9, C, C), (9 * C) ** -0.5, 0.0546875, ((1, 16), (2, 2))),
        "b_conv": scatter_about(arg_keys[8], (C,), 0.5, 3.0, ((0, 2),), jnp.float32),
    }


def convolve(image, w_conv):
    grid = image.astype(jnp.float32).reshape(C, HEIGHT, WIDTH)
    padded = jnp.pad(grid, ((0, 0), (1, 1), (1, 1)))
    total = jnp.zeros((C, HEIGHT * WIDTH), jnp.float32)
    for row_off in range(3):
        for col_off in range(3):
            window = padded[:, row_off:row_off + HEIGHT, col_off:col_off + WIDTH].reshape(C, HEIGHT * WIDTH)
            weights = w_conv[3 * row_off + col_off].astype(jnp.float32)
            total = total + jnp.einsum('io,ip->op', weights, window, precision=lax.Precision.HIGHEST)
    return total

def reference(h_in, skip, emb, w_emb, b_emb, gn_gain, gn_bias, w_conv, b_conv):
    act = jax.nn.silu(emb.astype(jnp.float32)).astype(jnp.bfloat16)
    shift = jnp.dot(act, w_emb, preferred_element_type=jnp.float32) + b_emb
    hidden = h_in.astype(jnp.float32) + shift[:, :, None]
    grouped = hidden.reshape(BATCH, GROUPS, C // GROUPS, HEIGHT * WIDTH)
    mean = lax.optimization_barrier(jnp.mean(grouped, axis=(2, 3), keepdims=True))
    var = lax.optimization_barrier(jnp.mean((grouped - mean) ** 2, axis=(2, 3), keepdims=True))
    scaled = ((grouped - mean) * lax.rsqrt(var + 1e-05)).reshape(BATCH, C, HEIGHT * WIDTH)
    normed = jax.nn.silu(scaled * gn_gain[:, None] + gn_bias[:, None]).astype(jnp.bfloat16)
    conv = lax.map(lambda image: convolve(image, w_conv), normed)
    conv = conv + b_conv[None, :, None]
    return (skip.astype(jnp.float32) + conv).astype(jnp.bfloat16)
```

```python
import functools

import jax
import jax.numpy as jnp
import numpy as np
from jax import lax
from jax.experimental import pallas as pl
from jax.experimental.pallas import tpu as pltpu
from jax.sharding import PartitionSpec as P

C = 1280
GROUPS = 32
HEIGHT = 32
WIDTH = 32
CELLS = HEIGHT * WIDTH
PADDED = CELLS + 2 * WIDTH
TILE = 256
ANY = pl.BlockSpec(memory_space=pl.ANY)


def chip_order(chips):
    if chips % 2:
        return list(range(chips))
    half = chips // 2
    return [2 * z for z in range(half)] + [2 * z + 1 for z in reversed(range(half))]


class Ring:
    def __init__(self, dp):
        self.dp = dp
        self.chips = dp // 2
        self.order = chip_order(self.chips)
        self.core_pairs = [(i, i ^ 1) for i in range(dp)]
        n, order = self.chips, self.order
        self.pairs = [(2 * order[k], 2 * order[(k + 1) % n]) for k in range(n)]
        self.pairs += [(2 * order[k] + 1, 2 * order[(k - 1) % n] + 1) for k in range(n)]
        full = (n - 1) // 2
        self.hops = [(s, h) for s in range(1, full + 1) for h in range(2)]
        if n % 2 == 0:
            self.hops.append((full + 1, 0))
        self.blocks = np.zeros((dp, dp), np.int32)
        for k in range(n):
            for core in range(2):
                me = 2 * order[k] + core
                units = [me, me ^ 1]
                for s, h in self.hops:
                    for c in (core, 1 - core):
                        chip = order[(k - s) % n] if c == 0 else order[(k + s) % n]
                        units.append(2 * chip + (c if h == 0 else 1 - c))
                self.blocks[me] = units
        self.places = np.argsort(self.blocks, axis=1).astype(np.int32)


def norm_kernel(place_ref, h_ref, ab_ref, *rest):
    x_ref = rest[-1]
    ab = ab_ref[0]
    v = h_ref[0].astype(jnp.float32) * ab[:, 0:1] + ab[:, 1:2]
    normed = v / (1.0 + jnp.exp(-v))
    column = lax.broadcasted_iota(jnp.int32, normed.shape, 1) % WIDTH
    left = jnp.where(column > 0, pltpu.roll(normed, 1, 1), 0.0)
    right = jnp.where(column < WIDTH - 1, pltpu.roll(normed, CELLS - 1, 1), 0.0)
    stack = jnp.concatenate([left, normed, right], axis=0)
    edge = jnp.zeros((WIDTH, x_ref.shape[2]), jnp.bfloat16)
    x_ref[0, :WIDTH, :] = edge
    x_ref[0, WIDTH + CELLS :, :] = edge
    x_ref[0, WIDTH : WIDTH + CELLS, :] = stack.T.astype(jnp.bfloat16)


def norm_call(units, places, h, ab, windows):
    blocks, rows, _ = h.shape
    shape = jax.ShapeDtypeStruct((units, PADDED, 3 * rows), jnp.bfloat16)
    more = () if windows is None else (windows,)
    return pl.pallas_call(
        norm_kernel,
        grid_spec=pltpu.PrefetchScalarGridSpec(
            num_scalar_prefetch=1,
            grid=(blocks,),
            in_specs=[
                pl.BlockSpec((1, rows, CELLS), lambda j, place: (j, 0, 0)),
                pl.BlockSpec((1, rows, 2), lambda j, place: (j, 0, 0)),
            ]
            + [ANY] * len(more),
            out_specs=pl.BlockSpec((1, PADDED, 3 * rows), lambda j, place: (place[j], 0, 0)),
        ),
        out_shape=shape,
        input_output_aliases={3: 0} if more else {},
        cost_estimate=pl.CostEstimate(
            flops=20 * blocks * rows * CELLS,
            transcendentals=2 * blocks * rows * CELLS,
            bytes_accessed=8 * blocks * rows * CELLS,
        ),
        name="norm_windows",
    )(places, h, ab, *more)


def conv_kernel(count, first, last, *refs):
    start = first == 0
    total_ref, x_ref = refs[:2]
    weight_refs = refs[2 : 2 + count]
    rest = refs[2 + count :]
    if last:
        skip_ref, rest = rest[0], rest[1:]
    out_ref, xs, ws, total, x_sem, w_sem, in_sem, out_sem = rest
    tiles = CELLS // TILE
    x_copies = [pltpu.make_async_copy(x_ref.at[first + u], xs.at[u], x_sem.at[u]) for u in range(count)]
    w_copies = [pltpu.make_async_copy(weight_refs[u], ws.at[u], w_sem.at[u]) for u in range(count)]
    rows = [pl.ds(t * TILE, TILE) for t in range(tiles)]
    in_copies = [] if start else [
        pltpu.make_async_copy(total_ref.at[rows[t]], total.at[rows[t]], in_sem.at[t]) for t in range(tiles)
    ]
    out_copies = [] if last else [
        pltpu.make_async_copy(total.at[rows[t]], out_ref.at[rows[t]], out_sem.at[t]) for t in range(tiles)
    ]
    for u in range(count):
        w_copies[u].start()
        x_copies[u].start()
    for copy in in_copies:
        copy.start()
    for t in range(tiles):
        base = t * TILE
        part = total_ref[...] if start else None
        for u in range(count):
            if t == 0:
                w_copies[u].wait()
                x_copies[u].wait()
            for dy in range(3):
                window = xs[u, base + WIDTH * dy : base + WIDTH * dy + TILE, :]
                term = jnp.dot(window, ws[u, dy], preferred_element_type=jnp.float32)
                part = term if part is None else part + term
        if not start:
            in_copies[t].wait()
            part = part + total[base : base + TILE, :]
        if last:
            skipped = skip_ref[:, base : base + TILE].astype(jnp.float32)
            out_ref[:, base : base + TILE] = (skipped + part.T).astype(jnp.bfloat16)
        else:
            total[base : base + TILE, :] = part
            out_copies[t].start()
    for copy in out_copies:
        copy.wait()


def conv_call(first, total, windows, weights, skip=None):
    count = len(weights)
    _, depth, outs = weights[0].shape
    last = skip is not None
    whole = pl.BlockSpec(memory_space=pltpu.VMEM)
    start = first == 0
    out_shape = (
        jax.ShapeDtypeStruct((outs, CELLS), jnp.bfloat16) if last else jax.ShapeDtypeStruct((CELLS, outs), jnp.float32)
    )
    tiles = CELLS // TILE
    return pl.pallas_call(
        functools.partial(conv_kernel, count, first, last),
        out_shape=out_shape,
        in_specs=[whole if start else ANY, ANY] + [ANY] * count + [whole] * last,
        out_specs=whole if last else ANY,
        scratch_shapes=[
            pltpu.VMEM((count, PADDED, depth), jnp.bfloat16),
            pltpu.VMEM((count, 3, depth, outs), jnp.bfloat16),
            pltpu.VMEM((CELLS, outs), jnp.float32),
            pltpu.SemaphoreType.DMA((count,)),
            pltpu.SemaphoreType.DMA((count,)),
            pltpu.SemaphoreType.DMA((tiles,)),
            pltpu.SemaphoreType.DMA((tiles,)),
        ],
        input_output_aliases={0: 0} if not (start or last) else {},
        compiler_params=pltpu.CompilerParams(vmem_limit_bytes=36 * 2**20),
        cost_estimate=pl.CostEstimate(
            flops=2 * CELLS * 3 * depth * outs * count,
            transcendentals=0,
            bytes_accessed=2 * count * 3 * depth * outs + 8 * CELLS * outs,
        ),
        name="conv_units",
    )(total, windows, *weights, *([skip] if last else []))


def make_body(dp, chan):
    ring = Ring(dp)
    chan_pairs = [(i, (i + 1) % chan) for i in range(chan)]

    def body(h_in, skip, emb, w_emb, b_emb, gn_gain, gn_bias, w_conv, b_conv):
        panel = h_in.shape[1]
        rows, outs = w_conv.shape[1], w_conv.shape[2]
        blocks = panel // rows
        me = lax.axis_index("dp")
        side = lax.axis_index("chan")

        own = w_conv.reshape(3, 3 * rows, outs)
        other = lax.ppermute(own, "dp", ring.core_pairs)
        units = [own, other]
        moving = [own, other]
        for _, half in ring.hops:
            moving[half] = lax.ppermute(moving[half], "dp", ring.pairs)
            units.append(moving[half])
            units.append(lax.ppermute(moving[half], "dp", ring.core_pairs))

        slices = [h_in.reshape(blocks, rows, CELLS)]
        for _ in range(chan - 1):
            slices.append(lax.ppermute(slices[-1], "chan", chan_pairs))

        act = jax.nn.silu(emb.astype(jnp.float32)).astype(jnp.bfloat16)
        act_rows = lax.all_to_all(act.reshape(dp, rows), "dp", 0, 0, tiled=True)
        terms = jnp.dot(act_rows, w_emb, preferred_element_type=jnp.float32)
        shift = jnp.sum(lax.all_to_all(terms, "dp", 0, 0, tiled=True), axis=0) + b_emb

        values = h_in[0].astype(jnp.float32)
        channel_mean = jnp.mean(values, axis=1, keepdims=True)
        channel_var = jnp.mean((values - channel_mean) ** 2, axis=1)
        size = C // GROUPS
        centers = (channel_mean[:, 0] + shift).reshape(panel // size, size)
        mean = jnp.mean(centers, axis=1, keepdims=True)
        var = jnp.mean(channel_var.reshape(panel // size, size) + (centers - mean) ** 2, axis=1, keepdims=True)
        scale = jnp.broadcast_to(lax.rsqrt(var + 1e-05), centers.shape).reshape(panel) * gn_gain
        offset = (shift - jnp.broadcast_to(mean, centers.shape).reshape(panel)) * scale + gn_bias
        affines = [jnp.stack([scale, offset])]
        for _ in range(chan - 1):
            affines.append(lax.ppermute(affines[-1], "chan", chan_pairs))

        windows = None
        table = jnp.asarray(ring.places)
        for turn in range(chan):
            place = lax.dynamic_slice(table, (me, ((side - turn) % chan) * blocks), (1, blocks))[0]
            ab = affines[turn].T.reshape(blocks, rows, 2)
            windows = norm_call(dp, place, slices[turn], ab, windows)

        total = b_conv.reshape(1, outs)
        cuts = [0, 4, 8, 12, dp - 2, dp] if dp == 16 else list(range(0, dp, 4)) + [dp]
        for first, stop in zip(cuts[:-2], cuts[1:-1]):
            total = conv_call(first, total, windows, units[first:stop])
        first = cuts[-2]
        out = conv_call(first, total, windows, units[first:], skip[0])
        return out[None]

    return body


def solution(mesh):
    return jax.shard_map(
        make_body(mesh.shape["dp"], mesh.shape["chan"]),
        mesh=mesh,
        in_specs=(
            P("dp", "chan", None),
            P("dp", "chan", None),
            P("dp", None),
            P("dp", "chan"),
            P("chan"),
            P("chan"),
            P("chan"),
            P(None, "dp", "chan"),
            P("chan"),
        ),
        out_specs=P("dp", "chan", None),
        check_vma=False,
    )
```

```python
import functools

import jax
import jax.numpy as jnp
import numpy as np
from jax import lax
from jax.experimental import pallas as pl
from jax.experimental.pallas import tpu as pltpu
from jax.sharding import PartitionSpec as P

C = 1280
GROUPS = 32
HEIGHT = 32
WIDTH = 32
CELLS = HEIGHT * WIDTH
VMEM_BYTES = 28 * 2**20
ANY = pl.BlockSpec(memory_space=pl.ANY)
HBM = pl.BlockSpec(memory_space=pltpu.HBM)
WHOLE = pl.BlockSpec(memory_space=pltpu.VMEM)


def chip_order(chips):
    if chips % 2:
        return list(range(chips))
    half = chips // 2
    return [2 * z for z in range(half)] + [2 * z + 1 for z in reversed(range(half))]


class Ring:
    def __init__(self, dp):
        self.dp = dp
        n = dp // 2
        order = chip_order(n)
        self.core_pairs = [(i, i ^ 1) for i in range(dp)]
        self.pairs = [(2 * order[k], 2 * order[(k + 1) % n]) for k in range(n)]
        self.pairs += [(2 * order[k] + 1, 2 * order[(k - 1) % n] + 1) for k in range(n)]
        full = (n - 1) // 2
        self.hops = [(s, h) for s in range(1, full + 1) for h in range(2)]
        if n % 2 == 0:
            self.hops.append((full + 1, 0))
        self.blocks = np.zeros((dp, dp), np.int32)
        for k in range(n):
            for core in range(2):
                me = 2 * order[k] + core
                units = [me, me ^ 1]
                for s, h in self.hops:
                    for c in (core, 1 - core):
                        chip = order[(k - s) % n] if c == 0 else order[(k + s) % n]
                        units.append(2 * chip + (c if h == 0 else 1 - c))
                self.blocks[me] = units


def act_kernel(emb_ref, piece_ref, out_ref, passed_ref):
    del piece_ref, passed_ref
    v = emb_ref[...].astype(jnp.float32)
    act = (v / (1.0 + jnp.exp(-v))).astype(jnp.bfloat16)
    rows = out_ref.shape[2]
    for d in range(out_ref.shape[0]):
        out_ref[d] = act[:, d * rows : (d + 1) * rows]


def act_call(emb, count, piece):
    return pl.pallas_call(
        act_kernel,
        out_shape=(
            jax.ShapeDtypeStruct((count, 1, emb.shape[1] // count), jnp.bfloat16),
            jax.ShapeDtypeStruct(piece.shape, piece.dtype),
        ),
        in_specs=[WHOLE, ANY],
        out_specs=(WHOLE, ANY),
        input_output_aliases={1: 1},
        compiler_params=pltpu.CompilerParams(vmem_limit_bytes=VMEM_BYTES),
        name="act_rows",
    )(emb, piece)


def emb_kernel(act_ref, w_ref, piece_ref, out_ref, passed_ref):
    del piece_ref, passed_ref
    out_ref[:, 0, :] = jnp.dot(act_ref[:, 0, :], w_ref[...], preferred_element_type=jnp.float32)


def emb_call(act_rows, w_emb, piece):
    shape = (act_rows.shape[0], 1, w_emb.shape[1])
    return pl.pallas_call(
        emb_kernel,
        out_shape=(jax.ShapeDtypeStruct(shape, jnp.float32), jax.ShapeDtypeStruct(piece.shape, piece.dtype)),
        in_specs=[WHOLE, WHOLE, ANY],
        out_specs=(WHOLE, ANY),
        input_output_aliases={2: 1},
        compiler_params=pltpu.CompilerParams(vmem_limit_bytes=VMEM_BYTES),
        name="emb_terms",
    )(act_rows, w_emb, piece)


def stats_kernel(h_ref, *refs):
    out_ref = refs[-1]
    panel = h_ref.shape[0]
    step = 80 if panel % 80 == 0 else panel
    count = len(refs) - 1
    for i in range(count):
        out_ref[i : i + 1, :] = refs[i][...]
    means, variances = [], []
    for start in range(0, panel, step):
        values = h_ref[start : start + step, :].astype(jnp.float32)
        mean = jnp.mean(values, axis=1, keepdims=True)
        means.append(mean)
        variances.append(jnp.mean((values - mean) ** 2, axis=1, keepdims=True))
    for i, columns in ((count, means), (count + 1, variances)):
        column = jnp.concatenate(columns, axis=0)
        out_ref[i : i + 1, :] = jnp.broadcast_to(column, (panel, 128)).T[0:1, :]


def stats_call(h, rows):
    shape = jax.ShapeDtypeStruct((len(rows) + 2, h.shape[0]), jnp.float32)
    return pl.pallas_call(
        stats_kernel,
        out_shape=shape,
        in_specs=[WHOLE] * (1 + len(rows)),
        out_specs=WHOLE,
        compiler_params=pltpu.CompilerParams(vmem_limit_bytes=VMEM_BYTES),
        cost_estimate=pl.CostEstimate(flops=5 * h.size, transcendentals=0, bytes_accessed=2 * h.size),
        name="channel_stats",
    )(h, *[row.reshape(1, -1) for row in rows])


def affine_kernel(size, terms_ref, table_ref, out_ref):
    rows = out_ref.shape[2]
    b_emb, gain, bias, channel_mean, channel_var = (table_ref[i : i + 1, :] for i in range(5))
    shift = jnp.sum(terms_ref[...], axis=0) + b_emb
    width = shift.shape[1]
    group = lax.broadcasted_iota(jnp.int32, (width, width // size), 0) // size
    member = (group == lax.broadcasted_iota(jnp.int32, group.shape, 1)).astype(jnp.float32)

    def per_group(row):
        row = jnp.broadcast_to(row, (8, row.shape[1]))
        return jnp.dot(row, member, precision=lax.Precision.HIGHEST, preferred_element_type=jnp.float32) / size

    def per_channel(groups):
        back = (((1,), (1,)), ((), ()))
        spread = lax.dot_general(
            groups, member, back, precision=lax.Precision.HIGHEST, preferred_element_type=jnp.float32
        )
        return spread[0:1, :]

    center = channel_mean + shift
    mean = per_channel(per_group(center))
    var = per_group(channel_var + (center - mean) ** 2)
    scale = per_channel(lax.rsqrt(var + 1e-05)) * gain
    offset = (shift - mean) * scale + bias
    both = jnp.concatenate([scale, offset], axis=0)
    for d in range(out_ref.shape[0]):
        out_ref[d] = both[:, d * rows : (d + 1) * rows]


def affine_call(size, rows, terms, table):
    channels = terms.shape[2]
    return pl.pallas_call(
        functools.partial(affine_kernel, size),
        out_shape=jax.ShapeDtypeStruct((channels // rows, 2, rows), jnp.float32),
        in_specs=[WHOLE, WHOLE],
        out_specs=WHOLE,
        compiler_params=pltpu.CompilerParams(vmem_limit_bytes=VMEM_BYTES),
        name="affine",
    )(terms, table)


def shifted(values, amount):
    edge = jnp.zeros((values.shape[0], abs(amount)), values.dtype)
    if amount > 0:
        return jnp.concatenate([values[:, amount:], edge], axis=1)
    return jnp.concatenate([edge, values[:, :amount]], axis=1)


def conv_kernel(ids, turns, tile, first, last, passing, *refs):
    refs = list(refs)
    count = len(ids)
    place_ref = refs.pop(0)
    base_ref = refs.pop(0)
    bias_ref = refs.pop(0) if first else None
    h_refs = [refs.pop(0) for _ in range(turns)]
    ab_ref = refs.pop(0)
    weight_refs = [refs.pop(0) for _ in range(count - (passing == 2))]
    if passing == 2:
        weight_refs.append(refs[0])
    passing = min(passing, 1)
    del refs[:passing]
    out_ref = refs.pop(0)
    del refs[:passing]
    hs, ws, base, total, even, odd, h_sem, w_sem, in_sem, out_sem = refs[:10]
    stacks = (even, odd)
    result = refs[10] if last else total
    blocks, rows, _ = h_refs[0].shape
    outs = total.shape[0]
    tiles = outs // tile
    cuts = [pl.ds(t * tile, tile) for t in range(tiles)]
    w_copies = [pltpu.make_async_copy(weight_refs[u], ws.at[u], w_sem.at[u]) for u in range(count)]
    in_copies = [pltpu.make_async_copy(base_ref.at[c], base.at[c], in_sem.at[t]) for t, c in enumerate(cuts)]
    out_copies = [pltpu.make_async_copy(result.at[c], out_ref.at[c], out_sem.at[t]) for t, c in enumerate(cuts)]
    for u in range(count):
        place = place_ref[ids[u]]
        for turn in range(turns):

            @pl.when(place // blocks == turn)
            def _():
                pltpu.make_async_copy(h_refs[turn].at[place % blocks], hs.at[u], h_sem.at[u]).start()

    for copy in w_copies + in_copies:
        copy.start()
    column = lax.broadcasted_iota(jnp.int32, (1, CELLS), 1) % WIDTH
    inside = [(column > 0).astype(jnp.bfloat16), None, (column < WIDTH - 1).astype(jnp.bfloat16)]

    def build(u):
        ab = ab_ref[place_ref[ids[u]]].T
        v = hs[u].astype(jnp.float32) * ab[:, 0:1] + ab[:, 1:2]
        half = 0.5 * v
        normed = (half + half * jnp.tanh(half)).astype(jnp.bfloat16)
        for dx in range(3):
            moved = normed if dx == 1 else shifted(normed, dx - 1) * inside[dx]
            for dy in range(3):
                row = (3 * dy + dx) * rows
                stacks[u % 2][row : row + rows, :] = moved if dy == 1 else shifted(moved, WIDTH * (dy - 1))

    def product(u, here):
        weights = ws[u, :, :, here].reshape(9 * rows, here.stop - here.start)
        return lax.dot_general(
            weights, stacks[u % 2][...], (((0,), (0,)), ((), ())), preferred_element_type=jnp.float32
        )

    for u in range(count):
        pltpu.make_async_copy(h_refs[0].at[0], hs.at[u], h_sem.at[u]).wait()
    build(0)
    for copy in w_copies:
        copy.wait()
    for u in range(count - 1):
        build(u + 1)
        part = product(u, slice(0, outs))
        total[...] = part if u == 0 else part + total[...]
    for copy in in_copies:
        copy.wait()
    for t in range(tiles):
        here = slice(t * tile, (t + 1) * tile)
        part = product(count - 1, here) + base[here, :].astype(jnp.float32)
        if count > 1:
            part = part + total[here, :]
        if first:
            part = part + jnp.broadcast_to(bias_ref[:, here], (8, tile)).T[:, 0:1]
        result[here, :] = part.astype(result.dtype)
        out_copies[t].start()
    for copy in out_copies:
        copy.wait()


def conv_call(places, ids, base, bias, slices, affine, weights, last=False, passed=None):
    count, turns = len(ids), len(slices)
    rows = slices[0].shape[1]
    outs = weights[0].shape[2]
    first = bias is not None
    tile = 128 if outs % 128 == 0 else outs
    tiles = outs // tile
    out_shape = [jax.ShapeDtypeStruct((outs, CELLS), jnp.bfloat16 if last else jnp.float32)]
    operands = [places, base] + ([bias] if first else []) + list(slices) + [affine] + list(weights)
    specs = [pl.BlockSpec(memory_space=pltpu.SMEM), HBM] + [WHOLE] * first + [HBM] + [ANY] * (turns - 1) + [WHOLE]
    specs += [HBM if id == 0 else ANY for id in ids[: len(weights)]]
    aliases = {} if first or last else {1: 0}
    passing = 0
    if passed is not None:
        passing = 1 if len(weights) == count else 2
        aliases[len(operands)] = 1
        operands.append(passed)
        specs.append(ANY)
        out_shape.append(jax.ShapeDtypeStruct(passed.shape, passed.dtype))
    scratch = [
        pltpu.VMEM((count, rows, CELLS), jnp.bfloat16),
        pltpu.VMEM((count,) + weights[0].shape, jnp.bfloat16),
        pltpu.VMEM((outs, CELLS), base.dtype),
        pltpu.VMEM((outs, CELLS), jnp.float32),
        pltpu.VMEM((9 * rows, CELLS), jnp.bfloat16),
        pltpu.VMEM((9 * rows, CELLS), jnp.bfloat16),
        pltpu.SemaphoreType.DMA((count,)),
        pltpu.SemaphoreType.DMA((count,)),
        pltpu.SemaphoreType.DMA((tiles,)),
        pltpu.SemaphoreType.DMA((tiles,)),
    ]
    if last:
        scratch.append(pltpu.VMEM((outs, CELLS), jnp.bfloat16))
    return pl.pallas_call(
        functools.partial(conv_kernel, tuple(ids), turns, tile, first, last, passing),
        out_shape=out_shape,
        in_specs=specs,
        out_specs=[HBM] + [ANY] * (passed is not None),
        scratch_shapes=scratch,
        input_output_aliases=aliases,
        compiler_params=pltpu.CompilerParams(vmem_limit_bytes=VMEM_BYTES),
        cost_estimate=pl.CostEstimate(
            flops=2 * CELLS * 9 * rows * outs * count,
            transcendentals=count * rows * CELLS,
            bytes_accessed=2 * count * 9 * rows * outs + 8 * CELLS * outs,
        ),
        name="conv_units",
    )(*operands)


def make_body(dp, chan):
    ring = Ring(dp)
    chan_pairs = [(i, (i + 1) % chan) for i in range(chan)]

    def around(value):
        values = [value]
        for _ in range(chan - 1):
            values.append(lax.ppermute(values[-1], "chan", chan_pairs))
        return values

    def body(h_in, skip, emb, w_emb, b_emb, gn_gain, gn_bias, w_conv, b_conv):
        panel = h_in.shape[1]
        rows, outs = w_conv.shape[1], w_conv.shape[2]
        blocks = panel // rows
        me = lax.axis_index("dp")
        side = lax.axis_index("chan")

        own = w_conv.reshape(3, 3 * rows, outs)
        final = len(ring.hops) + 1
        pieces = {0: own, 1: lax.ppermute(own, "dp", ring.core_pairs)}
        pieces[2] = lax.ppermute(own, "dp", ring.pairs)

        table = stats_call(h_in[0], [b_emb, gn_gain, gn_bias])
        slices = around(h_in.reshape(blocks, rows, CELLS))

        act, pieces[1] = act_call(emb, dp, pieces[1])
        act_rows = lax.all_to_all(act, "dp", 0, 0, tiled=True)
        terms, pieces[2] = emb_call(act_rows, w_emb, pieces[2])
        terms = lax.all_to_all(terms, "dp", 0, 0, tiled=True)
        affine = jnp.concatenate(around(affine_call(C // GROUPS, rows, terms, table)), axis=0)

        block = lax.dynamic_slice(jnp.asarray(ring.blocks), (me, 0), (1, dp))[0]
        places = ((side - block // blocks) % chan) * blocks + block % blocks

        state = {"total": skip[0], "bias": b_conv.reshape(1, outs), "left": dp}
        units = [(0, own), (1, pieces[1])]

        def convolve(count, passed=None):
            here = [units.pop(0) for _ in range(min(count, len(units)))]
            ids, weights = [u for u, _ in here], [w for _, w in here]
            if passed is not None and len(ids) < count - 1:
                ids.append(passed[0])
            state["left"] -= len(ids)
            results = conv_call(
                places,
                ids,
                state["total"],
                state["bias"],
                slices,
                affine,
                weights,
                state["left"] == 0,
                None if passed is None else passed[1],
            )
            state.update(total=results[0], bias=None)
            return results[-1], len(ids) > len(weights)

        for i in range(2, final + 1):
            if i > 2:
                pieces[i] = lax.ppermute(pieces[i - 2], "dp", ring.pairs)
            done = False
            if 4 <= i <= final - 2:
                pieces[i], done = convolve(4, (2 * i - 2, pieces[i]))
            if i == final:
                while units:
                    convolve(4)
            if not done:
                units.append((2 * i - 2, pieces[i]))
            units.append((2 * i - 1, lax.ppermute(pieces[i], "dp", ring.core_pairs)))
        while units:
            convolve(4)
        return state["total"][None]

    return body


def solution(mesh):
    return jax.shard_map(
        make_body(mesh.shape["dp"], mesh.shape["chan"]),
        mesh=mesh,
        in_specs=(
            P("dp", "chan", None),
            P("dp", "chan", None),
            P("dp", None),
            P("dp", "chan"),
            P("chan"),
            P("chan"),
            P("chan"),
            P(None, "dp", "chan"),
            P("chan"),
        ),
        out_specs=P("dp", "chan", None),
        check_vma=False,
    )
```

```python
import functools

import jax
import jax.numpy as jnp
import numpy as np
from jax import lax
from jax.experimental import pallas as pl
from jax.experimental.pallas import tpu as pltpu
from jax.sharding import PartitionSpec as P

C = 1280
GROUPS = 32
HEIGHT = 32
WIDTH = 32
CELLS = HEIGHT * WIDTH
VMEM_BYTES = 28 * 2**20
ANY = pl.BlockSpec(memory_space=pl.ANY)
WHOLE = pl.BlockSpec(memory_space=pltpu.VMEM)


def chip_order(chips):
    if chips % 2:
        return list(range(chips))
    half = chips // 2
    return [2 * z for z in range(half)] + [2 * z + 1 for z in reversed(range(half))]


class Ring:
    def __init__(self, dp):
        self.dp = dp
        n = dp // 2
        order = chip_order(n)
        self.core_pairs = [(i, i ^ 1) for i in range(dp)]
        self.pairs = [(2 * order[k], 2 * order[(k + 1) % n]) for k in range(n)]
        self.pairs += [(2 * order[k] + 1, 2 * order[(k - 1) % n] + 1) for k in range(n)]
        full = (n - 1) // 2
        self.hops = [(s, h) for s in range(1, full + 1) for h in range(2)]
        if n % 2 == 0:
            self.hops.append((full + 1, 0))
        self.blocks = np.zeros((dp, dp), np.int32)
        for k in range(n):
            for core in range(2):
                me = 2 * order[k] + core
                units = [me, me ^ 1]
                for s, h in self.hops:
                    for c in (core, 1 - core):
                        chip = order[(k - s) % n] if c == 0 else order[(k + s) % n]
                        units.append(2 * chip + (c if h == 0 else 1 - c))
                self.blocks[me] = units


def weight(times):
    return pl.CostEstimate(flops=times * 10**9, transcendentals=0, bytes_accessed=times * 4 * 10**6)


def nothing(*refs):
    del refs


def gate(piece, *others):
    return pl.pallas_call(
        nothing,
        out_shape=jax.ShapeDtypeStruct(piece.shape, piece.dtype),
        in_specs=[ANY] * (1 + len(others)),
        out_specs=ANY,
        input_output_aliases={0: 0},
        compiler_params=pltpu.CompilerParams(vmem_limit_bytes=2**20),
        name="gate",
    )(piece, *others)


def act_kernel(emb_ref, out_ref):
    v = emb_ref[...].astype(jnp.float32)
    act = (v / (1.0 + jnp.exp(-v))).astype(jnp.bfloat16)
    rows = out_ref.shape[2]
    for d in range(out_ref.shape[0]):
        out_ref[d] = act[:, d * rows : (d + 1) * rows]


def act_call(emb, count):
    return pl.pallas_call(
        act_kernel,
        out_shape=jax.ShapeDtypeStruct((count, 1, emb.shape[1] // count), jnp.bfloat16),
        in_specs=[WHOLE],
        out_specs=WHOLE,
        compiler_params=pltpu.CompilerParams(vmem_limit_bytes=VMEM_BYTES),
        name="act_rows",
    )(emb)


def emb_kernel(act_ref, w_ref, out_ref):
    out_ref[:, 0, :] = jnp.dot(act_ref[:, 0, :], w_ref[...], preferred_element_type=jnp.float32)


def emb_call(act_rows, w_emb):
    return pl.pallas_call(
        emb_kernel,
        out_shape=jax.ShapeDtypeStruct((act_rows.shape[0], 1, w_emb.shape[1]), jnp.float32),
        in_specs=[WHOLE, WHOLE],
        out_specs=WHOLE,
        compiler_params=pltpu.CompilerParams(vmem_limit_bytes=VMEM_BYTES),
        name="emb_terms",
    )(act_rows, w_emb)


def stats_kernel(h_ref, params_ref, out_ref):
    panel = h_ref.shape[0]
    step = 80 if panel % 80 == 0 else panel
    count = params_ref.shape[0]
    out_ref[0:count, :] = params_ref[...]
    means, variances = [], []
    for start in range(0, panel, step):
        values = h_ref[start : start + step, :].astype(jnp.float32)
        mean = jnp.mean(values, axis=1, keepdims=True)
        means.append(mean)
        variances.append(jnp.mean((values - mean) ** 2, axis=1, keepdims=True))
    for i, columns in ((count, means), (count + 1, variances)):
        column = jnp.concatenate(columns, axis=0)
        out_ref[i : i + 1, :] = jnp.broadcast_to(column, (panel, 128)).T[0:1, :]


def stats_call(h, params):
    return pl.pallas_call(
        stats_kernel,
        out_shape=jax.ShapeDtypeStruct((params.shape[0] + 2, h.shape[0]), jnp.float32),
        in_specs=[WHOLE, WHOLE],
        out_specs=WHOLE,
        compiler_params=pltpu.CompilerParams(vmem_limit_bytes=VMEM_BYTES),
        cost_estimate=weight(10),
        name="channel_stats",
    )(h, params)


def start_kernel(skip_ref, bias_ref, after_ref, out_ref):
    del after_ref
    outs = skip_ref.shape[0]
    bias = jnp.broadcast_to(bias_ref[...], (128, outs)).T[:, 0:1]
    out_ref[...] = skip_ref[...].astype(jnp.float32) + bias


def start_call(skip, bias, after):
    return pl.pallas_call(
        start_kernel,
        out_shape=jax.ShapeDtypeStruct(skip.shape, jnp.float32),
        in_specs=[WHOLE, WHOLE, ANY],
        out_specs=WHOLE,
        compiler_params=pltpu.CompilerParams(vmem_limit_bytes=VMEM_BYTES),
        cost_estimate=weight(0),
        name="start_total",
    )(skip, bias, after)


def affine_kernel(size, terms_ref, table_ref, *refs):
    out_ref = refs[-1]
    rows = out_ref.shape[2]
    b_emb, gain, bias, _, channel_mean, channel_var = (table_ref[i : i + 1, :] for i in range(6))
    shift = jnp.sum(terms_ref[...], axis=0) + b_emb
    width = shift.shape[1]
    group = lax.broadcasted_iota(jnp.int32, (width, width // size), 0) // size
    member = (group == lax.broadcasted_iota(jnp.int32, group.shape, 1)).astype(jnp.float32)

    def per_group(row):
        row = jnp.broadcast_to(row, (8, row.shape[1]))
        return jnp.dot(row, member, precision=lax.Precision.HIGHEST, preferred_element_type=jnp.float32) / size

    def per_channel(groups):
        back = (((1,), (1,)), ((), ()))
        spread = lax.dot_general(
            groups, member, back, precision=lax.Precision.HIGHEST, preferred_element_type=jnp.float32
        )
        return spread[0:1, :]

    center = channel_mean + shift
    mean = per_channel(per_group(center))
    var = per_group(channel_var + (center - mean) ** 2)
    scale = per_channel(lax.rsqrt(var + 1e-05)) * gain
    offset = (shift - mean) * scale + bias
    both = jnp.concatenate([scale, offset], axis=0)
    for d in range(out_ref.shape[0]):
        out_ref[d] = both[:, d * rows : (d + 1) * rows]


def affine_call(size, rows, terms, table, *after):
    channels = terms.shape[2]
    return pl.pallas_call(
        functools.partial(affine_kernel, size),
        out_shape=jax.ShapeDtypeStruct((channels // rows, 2, rows), jnp.float32),
        in_specs=[WHOLE, WHOLE] + [ANY] * len(after),
        out_specs=WHOLE,
        compiler_params=pltpu.CompilerParams(vmem_limit_bytes=VMEM_BYTES),
        cost_estimate=weight(10),
        name="affine",
    )(terms, table, *after)


def norm_kernel(place_ref, ab_ref, *refs):
    h_refs, out_ref = refs[:-1], refs[-1]
    blocks = h_refs[0].shape[0]
    for u in range(out_ref.shape[0]):
        place = place_ref[u]
        ab = ab_ref[place].T
        h = h_refs[0][place % blocks]
        for turn in range(1, len(h_refs)):
            h = jnp.where(place // blocks == turn, h_refs[turn][place % blocks], h)
        v = h.astype(jnp.float32) * ab[:, 0:1] + ab[:, 1:2]
        half = 0.5 * v
        out_ref[u] = (half + half * jnp.tanh(half)).astype(jnp.bfloat16)


def norm_call(places, affine, slices):
    return pl.pallas_call(
        norm_kernel,
        out_shape=jax.ShapeDtypeStruct(places.shape + slices[0].shape[1:], jnp.bfloat16),
        in_specs=[pl.BlockSpec(memory_space=pltpu.SMEM)] + [WHOLE] * (1 + len(slices)),
        out_specs=WHOLE,
        compiler_params=pltpu.CompilerParams(vmem_limit_bytes=VMEM_BYTES),
        cost_estimate=weight(0),
        name="norm_units",
    )(places, affine, *slices)


def shifted(values, amount):
    edge = jnp.zeros((values.shape[0], abs(amount)), values.dtype)
    if amount > 0:
        return jnp.concatenate([values[:, amount:], edge], axis=1)
    return jnp.concatenate([edge, values[:, :amount]], axis=1)


def conv_kernel(ids, last, *refs):
    count = len(ids)
    total_ref, normed_ref = refs[:2]
    weight_refs = refs[2 : 2 + count]
    out_ref, token_ref, even, odd, rounded, sem = refs[2 + count :]
    stacks = (even, odd)
    rows = normed_ref.shape[1]
    outs = total_ref.shape[0]
    column = lax.broadcasted_iota(jnp.int32, (1, CELLS), 1) % WIDTH
    inside = [(column > 0).astype(jnp.bfloat16), None, (column < WIDTH - 1).astype(jnp.bfloat16)]
    token_ref[...] = jnp.zeros_like(token_ref)

    def build(u):
        normed = normed_ref[ids[u]]
        for dx in range(3):
            moved = normed if dx == 1 else shifted(normed, dx - 1) * inside[dx]
            for dy in range(3):
                row = (3 * dy + dx) * rows
                stacks[u % 2][row : row + rows, :] = moved if dy == 1 else shifted(moved, WIDTH * (dy - 1))

    def product(u, here):
        weights = weight_refs[u][:, :, here].reshape(9 * rows, here.stop - here.start)
        return lax.dot_general(
            weights, stacks[u % 2][...], (((0,), (0,)), ((), ())), preferred_element_type=jnp.float32
        )

    build(0)
    if not last:
        for u in range(count):
            if u + 1 < count:
                build(u + 1)
            source = total_ref if u == 0 else out_ref
            out_ref[...] = source[...] + product(u, slice(0, outs))
        return
    tile = 128 if outs % 128 == 0 else outs
    copies = []
    for start in range(0, outs, tile):
        here = slice(start, start + tile)
        rounded[here, :] = (total_ref[here, :] + product(0, here)).astype(jnp.bfloat16)
        part = pl.ds(start, tile)
        copies.append(pltpu.make_async_copy(rounded.at[part], out_ref.at[part], sem.at[start // tile]))
        copies[-1].start()
    for copy in copies:
        copy.wait()


def conv_call(ids, total, normed, weights, last=False):
    count = len(ids)
    _, rows, _ = normed.shape
    outs = weights[0].shape[2]
    tiles = outs // 128 if outs % 128 == 0 else 1
    return pl.pallas_call(
        functools.partial(conv_kernel, tuple(ids), last),
        out_shape=[
            jax.ShapeDtypeStruct((outs, CELLS), jnp.bfloat16 if last else jnp.float32),
            jax.ShapeDtypeStruct((8, 128), jnp.float32),
        ],
        in_specs=[WHOLE] * (2 + count),
        out_specs=[ANY if last else WHOLE, WHOLE],
        scratch_shapes=[
            pltpu.VMEM((9 * rows, CELLS), jnp.bfloat16),
            pltpu.VMEM((9 * rows, CELLS), jnp.bfloat16),
            pltpu.VMEM((outs, CELLS) if last else (16, 128), jnp.bfloat16),
            pltpu.SemaphoreType.DMA((tiles,)),
        ],
        input_output_aliases={} if last else {0: 0},
        compiler_params=pltpu.CompilerParams(vmem_limit_bytes=VMEM_BYTES),
        name="conv_units",
    )(total, normed, *weights)


def make_body(dp, chan):
    ring = Ring(dp)
    chan_pairs = [(i, (i + 1) % chan) for i in range(chan)]

    def around(value):
        values = [value]
        for _ in range(chan - 1):
            values.append(lax.ppermute(values[-1], "chan", chan_pairs))
        return values

    def body(h_in, skip, emb, w_emb, b_emb, gn_gain, gn_bias, w_conv, b_conv):
        panel = h_in.shape[1]
        rows, outs = w_conv.shape[1], w_conv.shape[2]
        blocks = panel // rows
        me = lax.axis_index("dp")
        side = lax.axis_index("chan")

        own = w_conv.reshape(3, 3 * rows, outs)
        final = len(ring.hops) + 1
        pieces = {0: own, 1: lax.ppermute(own, "dp", ring.core_pairs)}
        pieces[2] = lax.ppermute(own, "dp", ring.pairs)

        slices = around(h_in.reshape(blocks, rows, CELLS))

        block = lax.dynamic_slice(jnp.asarray(ring.blocks), (me, 0), (1, dp))[0]
        places = ((side - block // blocks) % chan) * blocks + block % blocks

        def hop(i, *after):
            if after:
                pieces[i - 2] = gate(pieces[i - 2], *after)
            pieces[i] = lax.ppermute(pieces[i - 2], "dp", ring.pairs)

        act = act_call(emb, dp)
        act_rows = lax.all_to_all(act, "dp", 0, 0, tiled=True)
        params = jnp.concatenate([b_emb, gn_gain, gn_bias, b_conv]).reshape(4, panel)
        table = stats_call(h_in[0], params)
        if final >= 3:
            hop(3, act)
        terms = emb_call(act_rows, w_emb)
        total = start_call(skip[0], table[3:4], terms)
        if final >= 4:
            hop(4, terms)
        terms = lax.all_to_all(terms, "dp", 0, 0, tiled=True)
        affine = affine_call(C // GROUPS, rows, terms, table, total, places, pieces[min(3, final)], *slices[1:])
        affine = jnp.concatenate(around(affine), axis=0)
        if final >= 5:
            hop(5)

        normed = norm_call(places, affine, slices)

        units = [(0, own), (1, pieces[1])]
        tokens = []

        def arrived(i):
            units.append((2 * i - 2, pieces[i]))

        def swap(i):
            units.append((2 * i - 1, lax.ppermute(pieces[i], "dp", ring.core_pairs)))

        def convolve(total, count, last=False):
            here = [units.pop(0) for _ in range(min(count, len(units)))]
            total, token = conv_call([u for u, _ in here], total, normed, [w for _, w in here], last)
            tokens.append(token)
            return total

        for i in range(2, min(final, 3) + 1):
            arrived(i)
            swap(i)
        if final >= 4:
            total = convolve(total, 4)
        for i in range(6, final + 1):
            hop(i, tokens[-2] if len(tokens) > 1 else normed)
            arrived(i - 2)
            total = convolve(total, 4)
            swap(i - 2)
        if final >= 5:
            arrived(final - 1)
        while len(units) > 4:
            total = convolve(total, 4)
        if final >= 4:
            total = convolve(total, len(units))
            if final >= 5:
                swap(final - 1)
            pieces[final] = gate(pieces[final], tokens[-1])
            arrived(final)
            swap(final)
        while len(units) > 1:
            total = convolve(total, min(4, len(units) - 1))
        total = convolve(total, 1, last=True)
        return total[None]

    return body


def solution(mesh):
    return jax.shard_map(
        make_body(mesh.shape["dp"], mesh.shape["chan"]),
        mesh=mesh,
        in_specs=(
            P("dp", "chan", None),
            P("dp", "chan", None),
            P("dp", None),
            P("dp", "chan"),
            P("chan"),
            P("chan"),
            P("chan"),
            P(None, "dp", "chan"),
            P("chan"),
        ),
        out_specs=P("dp", "chan", None),
        check_vma=False,
    )
```

```python
import functools

import jax
import jax.numpy as jnp
import numpy as np
from jax import lax
from jax.experimental import pallas as pl
from jax.experimental.pallas import tpu as pltpu
from jax.sharding import PartitionSpec as P

C = 1280
GROUPS = 32
HEIGHT = 32
WIDTH = 32
CELLS = HEIGHT * WIDTH
VMEM_BYTES = 28 * 2**20
ANY = pl.BlockSpec(memory_space=pl.ANY)
WHOLE = pl.BlockSpec(memory_space=pltpu.VMEM)


def chip_order(chips):
    if chips % 2:
        return list(range(chips))
    half = chips // 2
    return [2 * z for z in range(half)] + [2 * z + 1 for z in reversed(range(half))]


class Ring:
    def __init__(self, dp):
        self.dp = dp
        n = dp // 2
        order = chip_order(n)
        self.core_pairs = [(i, i ^ 1) for i in range(dp)]
        self.pairs = [(2 * order[k], 2 * order[(k + 1) % n]) for k in range(n)]
        self.pairs += [(2 * order[k] + 1, 2 * order[(k - 1) % n] + 1) for k in range(n)]
        full = (n - 1) // 2
        self.hops = [(s, h) for s in range(1, full + 1) for h in range(2)]
        if n % 2 == 0:
            self.hops.append((full + 1, 0))
        self.blocks = np.zeros((dp, dp), np.int32)
        for k in range(n):
            for core in range(2):
                me = 2 * order[k] + core
                units = [me, me ^ 1]
                for s, h in self.hops:
                    for c in (core, 1 - core):
                        chip = order[(k - s) % n] if c == 0 else order[(k + s) % n]
                        units.append(2 * chip + (c if h == 0 else 1 - c))
                self.blocks[me] = units


def weight(times):
    return pl.CostEstimate(flops=times * 10**9, transcendentals=0, bytes_accessed=times * 4 * 10**6)


def nothing(*refs):
    del refs


def gate(piece, *others):
    return pl.pallas_call(
        nothing,
        out_shape=jax.ShapeDtypeStruct(piece.shape, piece.dtype),
        in_specs=[ANY] * (1 + len(others)),
        out_specs=ANY,
        input_output_aliases={0: 0},
        compiler_params=pltpu.CompilerParams(vmem_limit_bytes=2**20),
        name="gate",
    )(piece, *others)


def act_kernel(emb_ref, *refs):
    out_ref = refs[-1]
    v = emb_ref[...].astype(jnp.float32)
    act = (v / (1.0 + jnp.exp(-v))).astype(jnp.bfloat16)
    rows = out_ref.shape[2]
    for d in range(out_ref.shape[0]):
        out_ref[d] = act[:, d * rows : (d + 1) * rows]


def act_call(emb, count, *after):
    return pl.pallas_call(
        act_kernel,
        out_shape=jax.ShapeDtypeStruct((count, 1, emb.shape[1] // count), jnp.bfloat16),
        in_specs=[WHOLE] + [ANY] * len(after),
        out_specs=WHOLE,
        compiler_params=pltpu.CompilerParams(vmem_limit_bytes=VMEM_BYTES),
        name="act_rows",
    )(emb, *after)


def emb_kernel(act_ref, w_ref, out_ref):
    out_ref[:, 0, :] = jnp.dot(act_ref[:, 0, :], w_ref[...], preferred_element_type=jnp.float32)


def emb_call(act_rows, w_emb):
    return pl.pallas_call(
        emb_kernel,
        out_shape=jax.ShapeDtypeStruct((act_rows.shape[0], 1, w_emb.shape[1]), jnp.float32),
        in_specs=[WHOLE, WHOLE],
        out_specs=WHOLE,
        compiler_params=pltpu.CompilerParams(vmem_limit_bytes=VMEM_BYTES),
        name="emb_terms",
    )(act_rows, w_emb)


def stats_kernel(h_ref, params_ref, out_ref):
    panel = h_ref.shape[0]
    step = 80 if panel % 80 == 0 else panel
    count = params_ref.shape[0]
    out_ref[0:count, :] = params_ref[...]
    means, variances = [], []
    for start in range(0, panel, step):
        values = h_ref[start : start + step, :].astype(jnp.float32)
        mean = jnp.mean(values, axis=1, keepdims=True)
        means.append(mean)
        variances.append(jnp.mean((values - mean) ** 2, axis=1, keepdims=True))
    for i, columns in ((count, means), (count + 1, variances)):
        column = jnp.concatenate(columns, axis=0)
        out_ref[i : i + 1, :] = jnp.broadcast_to(column, (panel, 128)).T[0:1, :]


def stats_call(h, params):
    return pl.pallas_call(
        stats_kernel,
        out_shape=jax.ShapeDtypeStruct((params.shape[0] + 2, h.shape[0]), jnp.float32),
        in_specs=[WHOLE, WHOLE],
        out_specs=WHOLE,
        compiler_params=pltpu.CompilerParams(vmem_limit_bytes=VMEM_BYTES),
        cost_estimate=weight(10),
        name="channel_stats",
    )(h, params)


def affine_kernel(size, terms_ref, table_ref, *refs):
    out_ref = refs[-1]
    rows = out_ref.shape[2]
    b_emb, gain, bias, _, channel_mean, channel_var = (table_ref[i : i + 1, :] for i in range(6))
    shift = jnp.sum(terms_ref[...], axis=0) + b_emb
    width = shift.shape[1]
    group = lax.broadcasted_iota(jnp.int32, (width, width // size), 0) // size
    member = (group == lax.broadcasted_iota(jnp.int32, group.shape, 1)).astype(jnp.float32)

    def per_group(row):
        row = jnp.broadcast_to(row, (8, row.shape[1]))
        return jnp.dot(row, member, precision=lax.Precision.HIGHEST, preferred_element_type=jnp.float32) / size

    def per_channel(groups):
        back = (((1,), (1,)), ((), ()))
        spread = lax.dot_general(
            groups, member, back, precision=lax.Precision.HIGHEST, preferred_element_type=jnp.float32
        )
        return spread[0:1, :]

    center = channel_mean + shift
    mean = per_channel(per_group(center))
    var = per_group(channel_var + (center - mean) ** 2)
    scale = per_channel(lax.rsqrt(var + 1e-05)) * gain
    offset = (shift - mean) * scale + bias
    both = jnp.concatenate([scale, offset], axis=0)
    for d in range(out_ref.shape[0]):
        out_ref[d] = both[:, d * rows : (d + 1) * rows]


def affine_call(size, rows, terms, table, *after):
    channels = terms.shape[2]
    return pl.pallas_call(
        functools.partial(affine_kernel, size),
        out_shape=jax.ShapeDtypeStruct((channels // rows, 2, rows), jnp.float32),
        in_specs=[WHOLE, WHOLE] + [ANY] * len(after),
        out_specs=WHOLE,
        compiler_params=pltpu.CompilerParams(vmem_limit_bytes=VMEM_BYTES),
        cost_estimate=weight(5),
        name="affine",
    )(terms, table, *after)


def shifted(values, amount):
    edge = jnp.zeros((values.shape[0], abs(amount)), values.dtype)
    if amount > 0:
        return jnp.concatenate([values[:, amount:], edge], axis=1)
    return jnp.concatenate([edge, values[:, :amount]], axis=1)


def norm_kernel(units, chan, blocks_ref, ab_ref, *refs):
    h_refs, out_ref = refs[:-1], refs[-1]
    blocks = h_refs[0].shape[0]
    me, side = lax.axis_index("dp"), lax.axis_index("chan")
    for u in range(units):
        block = blocks_ref[me * units + u]
        turn, place = lax.rem(side - block // blocks + chan, chan), lax.rem(block, blocks)
        ab = ab_ref[turn * blocks + place].T
        h = h_refs[0][place]
        for other in range(1, chan):
            h = jnp.where(turn == other, h_refs[other][place], h)
        v = h.astype(jnp.float32) * ab[:, 0:1] + ab[:, 1:2]
        half = 0.5 * v
        out_ref[u] = (half + half * jnp.tanh(half)).astype(jnp.bfloat16)


def norm_call(blocks, affine, slices):
    units, chan = blocks.shape[0], len(slices)
    return pl.pallas_call(
        functools.partial(norm_kernel, units, chan),
        out_shape=jax.ShapeDtypeStruct((units,) + slices[0].shape[1:], jnp.bfloat16),
        in_specs=[pl.BlockSpec(memory_space=pltpu.SMEM)] + [WHOLE] * (1 + chan),
        out_specs=WHOLE,
        compiler_params=pltpu.CompilerParams(vmem_limit_bytes=VMEM_BYTES),
        cost_estimate=weight(0),
        name="norm_units",
    )(jnp.asarray(blocks.reshape(-1)), affine, *slices)


def conv_kernel(ids, first, extra, last, *refs):
    refs = list(refs)
    count = len(ids)
    total_ref = None if first else refs.pop(0)
    normed_ref = refs.pop(0)
    weight_refs = [refs.pop(0) for _ in range(count)]
    skip_ref, table_ref = (refs.pop(0), refs.pop(0)) if extra else (None, None)
    out_ref, token_ref, even, odd, rounded, sem = refs
    stacks = (even, odd)
    rows = normed_ref.shape[1]
    outs = out_ref.shape[0]
    column = lax.broadcasted_iota(jnp.int32, (1, CELLS), 1) % WIDTH
    inside = [(column > 0).astype(jnp.bfloat16), None, (column < WIDTH - 1).astype(jnp.bfloat16)]
    token_ref[...] = jnp.zeros_like(token_ref)

    def build(u):
        normed = normed_ref[ids[u]]
        for dx in range(3):
            moved = normed if dx == 1 else shifted(normed, dx - 1) * inside[dx]
            for dy in range(3):
                row = (3 * dy + dx) * rows
                stacks[u % 2][row : row + rows, :] = moved if dy == 1 else shifted(moved, WIDTH * (dy - 1))

    def product(u, here):
        weights = weight_refs[u][:, :, here].reshape(9 * rows, here.stop - here.start)
        return lax.dot_general(
            weights, stacks[u % 2][...], (((0,), (0,)), ((), ())), preferred_element_type=jnp.float32
        )

    build(0)
    if not last:
        for u in range(count):
            if u + 1 < count:
                build(u + 1)
            part = product(u, slice(0, outs))
            if u == 0 and extra:
                bias = jnp.broadcast_to(table_ref[3:4, :], (128, outs)).T[:, 0:1]
                part = part + (skip_ref[...].astype(jnp.float32) + bias)
            if not (u == 0 and first):
                part = part + (total_ref if u == 0 else out_ref)[...]
            out_ref[...] = part
        return
    tile = 128 if outs % 128 == 0 else outs
    copies = []
    for start in range(0, outs, tile):
        here = slice(start, start + tile)
        rounded[here, :] = (total_ref[here, :] + product(0, here)).astype(jnp.bfloat16)
        part = pl.ds(start, tile)
        copies.append(pltpu.make_async_copy(rounded.at[part], out_ref.at[part], sem.at[start // tile]))
        copies[-1].start()
    for copy in copies:
        copy.wait()


def conv_call(ids, total, normed, weights, extra=(), last=False):
    count, first = len(ids), total is None
    _, rows, _ = normed.shape
    outs = weights[0].shape[2]
    tiles = outs // 128 if outs % 128 == 0 else 1
    operands = ([] if first else [total]) + [normed] + list(weights) + list(extra)
    return pl.pallas_call(
        functools.partial(conv_kernel, tuple(ids), first, bool(extra), last),
        out_shape=[
            jax.ShapeDtypeStruct((outs, CELLS), jnp.bfloat16 if last else jnp.float32),
            jax.ShapeDtypeStruct((8, 128), jnp.float32),
        ],
        in_specs=[WHOLE] * len(operands),
        out_specs=[ANY if last else WHOLE, WHOLE],
        scratch_shapes=[
            pltpu.VMEM((9 * rows, CELLS), jnp.bfloat16),
            pltpu.VMEM((9 * rows, CELLS), jnp.bfloat16),
            pltpu.VMEM((outs, CELLS) if last else (16, 128), jnp.bfloat16),
            pltpu.SemaphoreType.DMA((tiles,)),
        ],
        input_output_aliases={} if first or last else {0: 0},
        compiler_params=pltpu.CompilerParams(vmem_limit_bytes=VMEM_BYTES),
        name="conv_units",
    )(*operands)


def make_body(dp, chan):
    ring = Ring(dp)
    chan_pairs = [(i, (i + 1) % chan) for i in range(chan)]

    def around(value):
        values = [value]
        for _ in range(chan - 1):
            values.append(lax.ppermute(values[-1], "chan", chan_pairs))
        return values

    def body(h_in, skip, emb, w_emb, b_emb, gn_gain, gn_bias, w_conv, b_conv):
        panel = h_in.shape[1]
        rows, outs = w_conv.shape[1], w_conv.shape[2]
        blocks = panel // rows

        own = w_conv.reshape(3, 3 * rows, outs)
        final = len(ring.hops) + 1
        pieces = {0: own, 1: lax.ppermute(own, "dp", ring.core_pairs)}
        pieces[2] = lax.ppermute(own, "dp", ring.pairs)

        slices = around(h_in.reshape(blocks, rows, CELLS))

        def hop(i, *after):
            if after:
                pieces[i - 2] = gate(pieces[i - 2], *after)
            pieces[i] = lax.ppermute(pieces[i - 2], "dp", ring.pairs)

        act = act_call(emb, dp, pieces[1])
        act_rows = lax.all_to_all(act, "dp", 0, 0, tiled=True)
        params = jnp.concatenate([b_emb, gn_gain, gn_bias, b_conv]).reshape(4, panel)
        table = stats_call(h_in[0], params)
        if final >= 3:
            hop(3, act)
        terms = emb_call(act_rows, w_emb)
        if final >= 4:
            hop(4, terms)
        terms = lax.all_to_all(terms, "dp", 0, 0, tiled=True)
        affine = affine_call(C // GROUPS, rows, terms, table, pieces[min(3, final)])
        affine = jnp.concatenate(around(affine), axis=0)
        if final >= 5:
            hop(5)

        normed = norm_call(ring.blocks, affine, slices)

        units = [(0, own), (1, pieces[1])]
        tokens = []

        def arrived(i):
            units.append((2 * i - 2, pieces[i]))

        def swap(i):
            units.append((2 * i - 1, lax.ppermute(pieces[i], "dp", ring.core_pairs)))

        def convolve(total, count, extra=(), last=False):
            here = [units.pop(0) for _ in range(min(count, len(units)))]
            total, token = conv_call([u for u, _ in here], total, normed, [w for _, w in here], extra, last)
            tokens.append(token)
            return total

        total = None
        for i in range(2, min(final, 3) + 1):
            arrived(i)
            swap(i)
        if final >= 4:
            total = convolve(total, 4)
        for i in range(6, final + 1):
            hop(i, ([normed, normed] + tokens)[i - 6])
            arrived(i - 2)
            total = convolve(total, 4)
            swap(i - 2)
        if final >= 5:
            arrived(final - 1)
        while len(units) > 4:
            total = convolve(total, 4)
        extra = (skip[0], table)
        if final >= 4:
            total = convolve(total, len(units), extra)
            extra = ()
            if final >= 5:
                swap(final - 1)
            pieces[final] = gate(pieces[final], tokens[-1])
            arrived(final)
            swap(final)
        while len(units) > 1:
            total = convolve(total, min(4, len(units) - 1), extra)
            extra = ()
        total = convolve(total, 1, extra, last=True)
        return total[None]

    return body


def solution(mesh):
    return jax.shard_map(
        make_body(mesh.shape["dp"], mesh.shape["chan"]),
        mesh=mesh,
        in_specs=(
            P("dp", "chan", None),
            P("dp", "chan", None),
            P("dp", None),
            P("dp", "chan"),
            P("chan"),
            P("chan"),
            P("chan"),
            P(None, "dp", "chan"),
            P("chan"),
        ),
        out_specs=P("dp", "chan", None),
        check_vma=False,
    )
```

```python
import functools

import jax
import jax.numpy as jnp
import numpy as np
from jax import lax
from jax.experimental import pallas as pl
from jax.experimental.pallas import tpu as pltpu
from jax.sharding import PartitionSpec as P

C = 1280
GROUPS = 32
HEIGHT = 32
WIDTH = 32
CELLS = HEIGHT * WIDTH
VMEM_BYTES = 28 * 2**20
ANY = pl.BlockSpec(memory_space=pl.ANY)
WHOLE = pl.BlockSpec(memory_space=pltpu.VMEM)


def chip_order(chips):
    if chips % 2:
        return list(range(chips))
    half = chips // 2
    return [2 * z for z in range(half)] + [2 * z + 1 for z in reversed(range(half))]


class Ring:
    def __init__(self, dp):
        self.dp = dp
        n = dp // 2
        order = chip_order(n)
        self.core_pairs = [(i, i ^ 1) for i in range(dp)]
        self.pairs = [(2 * order[k], 2 * order[(k + 1) % n]) for k in range(n)]
        self.pairs += [(2 * order[k] + 1, 2 * order[(k - 1) % n] + 1) for k in range(n)]
        full = (n - 1) // 2
        self.hops = [(s, h) for s in range(1, full + 1) for h in range(2)]
        if n % 2 == 0:
            self.hops.append((full + 1, 0))
        self.blocks = np.zeros((dp, dp), np.int32)
        for k in range(n):
            for core in range(2):
                me = 2 * order[k] + core
                units = [me, me ^ 1]
                for s, h in self.hops:
                    for c in (core, 1 - core):
                        chip = order[(k - s) % n] if c == 0 else order[(k + s) % n]
                        units.append(2 * chip + (c if h == 0 else 1 - c))
                self.blocks[me] = units


def weight(times):
    return pl.CostEstimate(flops=times * 10**9, transcendentals=0, bytes_accessed=times * 4 * 10**6)


def nothing(*refs):
    del refs


def gate(piece, *others):
    return pl.pallas_call(
        nothing,
        out_shape=jax.ShapeDtypeStruct(piece.shape, piece.dtype),
        in_specs=[ANY] * (1 + len(others)),
        out_specs=ANY,
        input_output_aliases={0: 0},
        compiler_params=pltpu.CompilerParams(vmem_limit_bytes=2**20),
        name="gate",
    )(piece, *others)


def act_kernel(emb_ref, *refs):
    out_ref = refs[-1]
    v = emb_ref[...].astype(jnp.float32)
    act = (v / (1.0 + jnp.exp(-v))).astype(jnp.bfloat16)
    rows = out_ref.shape[2]
    for d in range(out_ref.shape[0]):
        out_ref[d] = act[:, d * rows : (d + 1) * rows]


def act_call(emb, count, *after):
    return pl.pallas_call(
        act_kernel,
        out_shape=jax.ShapeDtypeStruct((count, 1, emb.shape[1] // count), jnp.bfloat16),
        in_specs=[WHOLE] + [ANY] * len(after),
        out_specs=WHOLE,
        compiler_params=pltpu.CompilerParams(vmem_limit_bytes=VMEM_BYTES),
        name="act_rows",
    )(emb, *after)


def emb_kernel(act_ref, w_ref, out_ref):
    out_ref[:, 0, :] = jnp.dot(act_ref[:, 0, :], w_ref[...], preferred_element_type=jnp.float32)


def emb_call(act_rows, w_emb):
    return pl.pallas_call(
        emb_kernel,
        out_shape=jax.ShapeDtypeStruct((act_rows.shape[0], 1, w_emb.shape[1]), jnp.float32),
        in_specs=[WHOLE, WHOLE],
        out_specs=WHOLE,
        compiler_params=pltpu.CompilerParams(vmem_limit_bytes=VMEM_BYTES),
        name="emb_terms",
    )(act_rows, w_emb)


def stats_kernel(h_ref, params_ref, out_ref):
    panel = h_ref.shape[0]
    step = 80 if panel % 80 == 0 else panel
    count = params_ref.shape[0]
    out_ref[0:count, :] = params_ref[...]
    means, variances = [], []
    for start in range(0, panel, step):
        values = h_ref[start : start + step, :].astype(jnp.float32)
        mean = jnp.mean(values, axis=1, keepdims=True)
        means.append(mean)
        variances.append(jnp.mean((values - mean) ** 2, axis=1, keepdims=True))
    for i, columns in ((count, means), (count + 1, variances)):
        column = jnp.concatenate(columns, axis=0)
        out_ref[i : i + 1, :] = jnp.broadcast_to(column, (panel, 128)).T[0:1, :]


def stats_call(h, params):
    return pl.pallas_call(
        stats_kernel,
        out_shape=jax.ShapeDtypeStruct((params.shape[0] + 2, h.shape[0]), jnp.float32),
        in_specs=[WHOLE, WHOLE],
        out_specs=WHOLE,
        compiler_params=pltpu.CompilerParams(vmem_limit_bytes=VMEM_BYTES),
        cost_estimate=weight(10),
        name="channel_stats",
    )(h, params)


def affine_kernel(size, terms_ref, table_ref, *refs):
    out_ref = refs[-1]
    rows = out_ref.shape[2]
    b_emb, gain, bias, _, channel_mean, channel_var = (table_ref[i : i + 1, :] for i in range(6))
    shift = jnp.sum(terms_ref[...], axis=0) + b_emb
    width = shift.shape[1]
    group = lax.broadcasted_iota(jnp.int32, (width, width // size), 0) // size
    member = (group == lax.broadcasted_iota(jnp.int32, group.shape, 1)).astype(jnp.float32)

    def per_group(row):
        row = jnp.broadcast_to(row, (8, row.shape[1]))
        return jnp.dot(row, member, precision=lax.Precision.HIGHEST, preferred_element_type=jnp.float32) / size

    def per_channel(groups):
        back = (((1,), (1,)), ((), ()))
        spread = lax.dot_general(
            groups, member, back, precision=lax.Precision.HIGHEST, preferred_element_type=jnp.float32
        )
        return spread[0:1, :]

    center = channel_mean + shift
    mean = per_channel(per_group(center))
    var = per_group(channel_var + (center - mean) ** 2)
    scale = per_channel(lax.rsqrt(var + 1e-05)) * gain
    offset = (shift - mean) * scale + bias
    both = jnp.concatenate([scale, offset], axis=0)
    for d in range(out_ref.shape[0]):
        out_ref[d] = both[:, d * rows : (d + 1) * rows]


def affine_call(size, rows, terms, table, *after):
    channels = terms.shape[2]
    return pl.pallas_call(
        functools.partial(affine_kernel, size),
        out_shape=jax.ShapeDtypeStruct((channels // rows, 2, rows), jnp.float32),
        in_specs=[WHOLE, WHOLE] + [ANY] * len(after),
        out_specs=WHOLE,
        compiler_params=pltpu.CompilerParams(vmem_limit_bytes=VMEM_BYTES),
        cost_estimate=weight(7),
        name="affine",
    )(terms, table, *after)


def shifted(values, amount):
    edge = jnp.zeros((values.shape[0], abs(amount)), values.dtype)
    if amount > 0:
        return jnp.concatenate([values[:, amount:], edge], axis=1)
    return jnp.concatenate([edge, values[:, :amount]], axis=1)


def norm_kernel(units, chan, blocks_ref, ab_ref, *refs):
    h_refs, out_ref = refs[:-1], refs[-1]
    blocks = h_refs[0].shape[0]
    me, side = lax.axis_index("dp"), lax.axis_index("chan")
    for u in range(units):
        block = blocks_ref[me * units + u]
        turn, place = lax.rem(side - block // blocks + chan, chan), lax.rem(block, blocks)
        ab = ab_ref[turn * blocks + place].T
        h = h_refs[0][place]
        for other in range(1, chan):
            h = jnp.where(turn == other, h_refs[other][place], h)
        v = h.astype(jnp.float32) * ab[:, 0:1] + ab[:, 1:2]
        half = 0.5 * v
        out_ref[u] = (half + half * jnp.tanh(half)).astype(jnp.bfloat16)


def norm_call(blocks, affine, slices):
    units, chan = blocks.shape[0], len(slices)
    return pl.pallas_call(
        functools.partial(norm_kernel, units, chan),
        out_shape=jax.ShapeDtypeStruct((units,) + slices[0].shape[1:], jnp.bfloat16),
        in_specs=[pl.BlockSpec(memory_space=pltpu.SMEM)] + [WHOLE] * (1 + chan),
        out_specs=WHOLE,
        compiler_params=pltpu.CompilerParams(vmem_limit_bytes=VMEM_BYTES),
        cost_estimate=weight(0),
        name="norm_units",
    )(jnp.asarray(blocks.reshape(-1)), affine, *slices)


def conv_kernel(parts, first, extra, last, *refs):
    refs = list(refs)
    count = len(parts)
    total_ref = None if first else refs.pop(0)
    normed_ref = refs.pop(0)
    weight_refs = [refs.pop(0) for _ in range(count)]
    skip_ref, table_ref = (refs.pop(0), refs.pop(0)) if extra else (None, None)
    out_ref, token_ref, even, odd, rounded, sem = refs
    stacks = (even, odd)
    rows = normed_ref.shape[1]
    outs = out_ref.shape[0]
    column = lax.broadcasted_iota(jnp.int32, (1, CELLS), 1) % WIDTH
    inside = [(column > 0).astype(jnp.bfloat16), None, (column < WIDTH - 1).astype(jnp.bfloat16)]
    token_ref[...] = jnp.zeros_like(token_ref)

    def build(u):
        unit, taps = parts[u]
        normed = normed_ref[unit]
        for dx in range(3):
            moved = normed if dx == 1 else shifted(normed, dx - 1) * inside[dx]
            for dy in taps:
                row = (3 * (dy - taps[0]) + dx) * rows
                stacks[u % 2][row : row + rows, :] = moved if dy == 1 else shifted(moved, WIDTH * (dy - 1))

    def product(u, here):
        depth = 3 * len(parts[u][1]) * rows
        weights = weight_refs[u][:, :, here].reshape(depth, here.stop - here.start)
        return lax.dot_general(
            weights, stacks[u % 2][:depth, :], (((0,), (0,)), ((), ())), preferred_element_type=jnp.float32
        )

    build(0)
    if not last:
        for u in range(count):
            if u + 1 < count:
                build(u + 1)
            part = product(u, slice(0, outs))
            if u == 0 and extra:
                bias = jnp.broadcast_to(table_ref[3:4, :], (128, outs)).T[:, 0:1]
                part = part + (skip_ref[...].astype(jnp.float32) + bias)
            if not (u == 0 and first):
                part = part + (total_ref if u == 0 else out_ref)[...]
            out_ref[...] = part
        return
    tile = 128 if outs % 128 == 0 else outs
    copies = []
    for start in range(0, outs, tile):
        here = slice(start, start + tile)
        rounded[here, :] = (total_ref[here, :] + product(0, here)).astype(jnp.bfloat16)
        part = pl.ds(start, tile)
        copies.append(pltpu.make_async_copy(rounded.at[part], out_ref.at[part], sem.at[start // tile]))
        copies[-1].start()
    for copy in copies:
        copy.wait()


def conv_call(parts, total, normed, weights, extra=(), last=False):
    first = total is None
    _, rows, _ = normed.shape
    outs = weights[0].shape[2]
    tiles = outs // 128 if outs % 128 == 0 else 1
    operands = ([] if first else [total]) + [normed] + list(weights) + list(extra)
    return pl.pallas_call(
        functools.partial(conv_kernel, tuple(parts), first, bool(extra), last),
        out_shape=[
            jax.ShapeDtypeStruct((outs, CELLS), jnp.bfloat16 if last else jnp.float32),
            jax.ShapeDtypeStruct((8, 128), jnp.float32),
        ],
        in_specs=[WHOLE] * len(operands),
        out_specs=[ANY if last else WHOLE, WHOLE],
        scratch_shapes=[
            pltpu.VMEM((9 * rows, CELLS), jnp.bfloat16),
            pltpu.VMEM((9 * rows, CELLS), jnp.bfloat16),
            pltpu.VMEM((outs, CELLS) if last else (16, 128), jnp.bfloat16),
            pltpu.SemaphoreType.DMA((tiles,)),
        ],
        input_output_aliases={} if first or last else {0: 0},
        compiler_params=pltpu.CompilerParams(vmem_limit_bytes=VMEM_BYTES),
        name="conv_units",
    )(*operands)


def make_body(dp, chan):
    ring = Ring(dp)
    chan_pairs = [(i, (i + 1) % chan) for i in range(chan)]

    def around(value):
        values = [value]
        for _ in range(chan - 1):
            values.append(lax.ppermute(values[-1], "chan", chan_pairs))
        return values

    def body(h_in, skip, emb, w_emb, b_emb, gn_gain, gn_bias, w_conv, b_conv):
        panel = h_in.shape[1]
        rows, outs = w_conv.shape[1], w_conv.shape[2]
        blocks = panel // rows

        own = w_conv.reshape(3, 3 * rows, outs)
        final = len(ring.hops) + 1
        pieces = {0: own, 1: lax.ppermute(own, "dp", ring.core_pairs)}
        pieces[2] = lax.ppermute(own, "dp", ring.pairs)

        slices = around(h_in.reshape(blocks, rows, CELLS))

        def hop(i, *after):
            if after:
                pieces[i - 2] = gate(pieces[i - 2], *after)
            pieces[i] = lax.ppermute(pieces[i - 2], "dp", ring.pairs)

        act = act_call(emb, dp, pieces[1])
        act_rows = lax.all_to_all(act, "dp", 0, 0, tiled=True)
        params = jnp.concatenate([b_emb, gn_gain, gn_bias, b_conv]).reshape(4, panel)
        table = stats_call(h_in[0], params)
        if final >= 3:
            hop(3, act)
        terms = emb_call(act_rows, w_emb)
        if final >= 4:
            hop(4, terms)
        terms = lax.all_to_all(terms, "dp", 0, 0, tiled=True)
        affine = affine_call(C // GROUPS, rows, terms, table, pieces[min(3, final)])
        affine = jnp.concatenate(around(affine), axis=0)
        if final >= 5:
            hop(5)

        normed = norm_call(ring.blocks, affine, slices)

        taps = tuple(range(3))
        units = [((0, taps), own), ((1, taps), pieces[1])]
        tokens = []

        def swapped(piece):
            return lax.ppermute(piece, "dp", ring.core_pairs)

        def arrived(i):
            units.append(((2 * i - 2, taps), pieces[i]))

        def swap(i):
            units.append(((2 * i - 1, taps), swapped(pieces[i])))

        def convolve(total, count, extra=(), last=False):
            here = [units.pop(0) for _ in range(min(count, len(units)))]
            total, token = conv_call([p for p, _ in here], total, normed, [w for _, w in here], extra, last)
            tokens.append(token)
            return total

        total = None
        for i in range(2, min(final, 3) + 1):
            arrived(i)
            swap(i)
        if final >= 4:
            total = convolve(total, 4)
        for i in range(6, final + 1):
            after = ([normed] + tokens)[i - 6]
            if i < final:
                hop(i, after)
            else:
                pieces[i - 2] = gate(pieces[i - 2], after)
                tail = [
                    (rows_of_taps, lax.ppermute(pieces[i - 2][rows_of_taps[0] : rows_of_taps[-1] + 1], "dp", ring.pairs))
                    for rows_of_taps in (taps[:2], taps[2:])
                ]
            arrived(i - 2)
            total = convolve(total, 4)
            swap(i - 2)
        if final >= 6:
            pieces[final - 1] = gate(pieces[final - 1], tokens[-1])
            arrived(final - 1)
        else:
            tail = []
            for i in range(4, final + 1):
                arrived(i)
                swap(i)
        while len(units) > 4:
            total = convolve(total, 4)
        extra = (skip[0], table)
        if tail:
            total = convolve(total, len(units), extra)
            extra = ()
            swap(final - 1)
        for rows_of_taps, piece in tail:
            piece = gate(piece, tokens[-1])
            units.append(((2 * final - 2, rows_of_taps), piece))
            moving = ((2 * final - 1, rows_of_taps), swapped(piece))
            total = convolve(total, len(units))
            units.append(moving)
        while len(units) > 1:
            total = convolve(total, min(4, len(units) - 1), extra)
            extra = ()
        total = convolve(total, 1, extra, last=True)
        return total[None]

    return body


def solution(mesh):
    return jax.shard_map(
        make_body(mesh.shape["dp"], mesh.shape["chan"]),
        mesh=mesh,
        in_specs=(
            P("dp", "chan", None),
            P("dp", "chan", None),
            P("dp", None),
            P("dp", "chan"),
            P("chan"),
            P("chan"),
            P("chan"),
            P(None, "dp", "chan"),
            P("chan"),
        ),
        out_specs=P("dp", "chan", None),
        check_vma=False,
    )
```

```python
import functools

import jax
import jax.numpy as jnp
import numpy as np
from jax import lax
from jax.experimental import pallas as pl
from jax.experimental.pallas import tpu as pltpu
from jax.sharding import PartitionSpec as P

C = 1280
GROUPS = 32
HEIGHT = 32
WIDTH = 32
CELLS = HEIGHT * WIDTH
VMEM_BYTES = 28 * 2**20
ANY = pl.BlockSpec(memory_space=pl.ANY)
WHOLE = pl.BlockSpec(memory_space=pltpu.VMEM)


def chip_order(chips):
    if chips % 2:
        return list(range(chips))
    half = chips // 2
    return [2 * z for z in range(half)] + [2 * z + 1 for z in reversed(range(half))]


class Ring:
    def __init__(self, dp):
        self.dp = dp
        n = dp // 2
        order = chip_order(n)
        self.core_pairs = [(i, i ^ 1) for i in range(dp)]
        self.pairs = [(2 * order[k], 2 * order[(k + 1) % n]) for k in range(n)]
        self.pairs += [(2 * order[k] + 1, 2 * order[(k - 1) % n] + 1) for k in range(n)]
        full = (n - 1) // 2
        self.hops = [(s, h) for s in range(1, full + 1) for h in range(2)]
        if n % 2 == 0:
            self.hops.append((full + 1, 0))
        self.blocks = np.zeros((dp, dp), np.int32)
        for k in range(n):
            for core in range(2):
                me = 2 * order[k] + core
                units = [me, me ^ 1]
                for s, h in self.hops:
                    for c in (core, 1 - core):
                        chip = order[(k - s) % n] if c == 0 else order[(k + s) % n]
                        units.append(2 * chip + (c if h == 0 else 1 - c))
                self.blocks[me] = units


def weight(times):
    return pl.CostEstimate(flops=int(times * 1e9), transcendentals=0, bytes_accessed=int(times * 4e6))


def nothing(*refs):
    del refs


def gate(piece, *others, times=None):
    return pl.pallas_call(
        nothing,
        out_shape=jax.ShapeDtypeStruct(piece.shape, piece.dtype),
        in_specs=[ANY] * (1 + len(others)),
        out_specs=ANY,
        input_output_aliases={0: 0},
        compiler_params=pltpu.CompilerParams(vmem_limit_bytes=2**20),
        cost_estimate=None if times is None else weight(times),
        name="gate",
    )(piece, *others)


def act_kernel(emb_ref, *refs):
    out_ref = refs[-1]
    v = emb_ref[...].astype(jnp.float32)
    act = (v / (1.0 + jnp.exp(-v))).astype(jnp.bfloat16)
    rows = out_ref.shape[2]
    for d in range(out_ref.shape[0]):
        out_ref[d] = act[:, d * rows : (d + 1) * rows]


def act_call(emb, count, *after):
    return pl.pallas_call(
        act_kernel,
        out_shape=jax.ShapeDtypeStruct((count, 1, emb.shape[1] // count), jnp.bfloat16),
        in_specs=[WHOLE] + [ANY] * len(after),
        out_specs=WHOLE,
        compiler_params=pltpu.CompilerParams(vmem_limit_bytes=VMEM_BYTES),
        name="act_rows",
    )(emb, *after)


def emb_kernel(act_ref, w_ref, out_ref):
    out_ref[:, 0, :] = jnp.dot(act_ref[:, 0, :], w_ref[...], preferred_element_type=jnp.float32)


def emb_call(act_rows, w_emb):
    return pl.pallas_call(
        emb_kernel,
        out_shape=jax.ShapeDtypeStruct((act_rows.shape[0], 1, w_emb.shape[1]), jnp.float32),
        in_specs=[WHOLE, WHOLE],
        out_specs=WHOLE,
        compiler_params=pltpu.CompilerParams(vmem_limit_bytes=VMEM_BYTES),
        name="emb_terms",
    )(act_rows, w_emb)


def stats_kernel(h_ref, params_ref, out_ref):
    panel = h_ref.shape[0]
    step = 80 if panel % 80 == 0 else panel
    count = params_ref.shape[0]
    out_ref[0:count, :] = params_ref[...]
    means, variances = [], []
    for start in range(0, panel, step):
        values = h_ref[start : start + step, :].astype(jnp.float32)
        mean = jnp.mean(values, axis=1, keepdims=True)
        means.append(mean)
        variances.append(jnp.mean((values - mean) ** 2, axis=1, keepdims=True))
    for i, columns in ((count, means), (count + 1, variances)):
        column = jnp.concatenate(columns, axis=0)
        out_ref[i : i + 1, :] = jnp.broadcast_to(column, (panel, 128)).T[0:1, :]


def stats_call(h, params):
    return pl.pallas_call(
        stats_kernel,
        out_shape=jax.ShapeDtypeStruct((params.shape[0] + 2, h.shape[0]), jnp.float32),
        in_specs=[WHOLE, WHOLE],
        out_specs=WHOLE,
        compiler_params=pltpu.CompilerParams(vmem_limit_bytes=VMEM_BYTES),
        cost_estimate=weight(10),
        name="channel_stats",
    )(h, params)


def affine_kernel(size, terms_ref, table_ref, *refs):
    out_ref = refs[-1]
    rows = out_ref.shape[2]
    b_emb, gain, bias, _, channel_mean, channel_var = (table_ref[i : i + 1, :] for i in range(6))
    shift = jnp.sum(terms_ref[...], axis=0) + b_emb
    width = shift.shape[1]
    group = lax.broadcasted_iota(jnp.int32, (width, width // size), 0) // size
    member = (group == lax.broadcasted_iota(jnp.int32, group.shape, 1)).astype(jnp.float32)

    def per_group(row):
        row = jnp.broadcast_to(row, (8, row.shape[1]))
        return jnp.dot(row, member, precision=lax.Precision.HIGHEST, preferred_element_type=jnp.float32) / size

    def per_channel(groups):
        back = (((1,), (1,)), ((), ()))
        spread = lax.dot_general(
            groups, member, back, precision=lax.Precision.HIGHEST, preferred_element_type=jnp.float32
        )
        return spread[0:1, :]

    center = channel_mean + shift
    mean = per_channel(per_group(center))
    var = per_group(channel_var + (center - mean) ** 2)
    scale = per_channel(lax.rsqrt(var + 1e-05)) * gain
    offset = (shift - mean) * scale + bias
    both = jnp.concatenate([scale, offset], axis=0)
    for d in range(out_ref.shape[0]):
        out_ref[d] = both[:, d * rows : (d + 1) * rows]


def affine_call(size, rows, terms, table, *after):
    channels = terms.shape[2]
    return pl.pallas_call(
        functools.partial(affine_kernel, size),
        out_shape=jax.ShapeDtypeStruct((channels // rows, 2, rows), jnp.float32),
        in_specs=[WHOLE, WHOLE] + [ANY] * len(after),
        out_specs=WHOLE,
        compiler_params=pltpu.CompilerParams(vmem_limit_bytes=VMEM_BYTES),
        cost_estimate=weight(7),
        name="affine",
    )(terms, table, *after)


def shifted(values, amount):
    edge = jnp.zeros((values.shape[0], abs(amount)), values.dtype)
    if amount > 0:
        return jnp.concatenate([values[:, amount:], edge], axis=1)
    return jnp.concatenate([edge, values[:, :amount]], axis=1)


def norm_kernel(units, chan, blocks_ref, ab_ref, *refs):
    h_refs, out_ref = refs[:-1], refs[-1]
    blocks = h_refs[0].shape[0]
    me, side = lax.axis_index("dp"), lax.axis_index("chan")
    for u in range(units):
        block = blocks_ref[me * units + u]
        turn, place = lax.rem(side - block // blocks + chan, chan), lax.rem(block, blocks)
        ab = ab_ref[turn * blocks + place].T
        h = h_refs[0][place]
        for other in range(1, chan):
            h = jnp.where(turn == other, h_refs[other][place], h)
        v = h.astype(jnp.float32) * ab[:, 0:1] + ab[:, 1:2]
        half = 0.5 * v
        out_ref[u] = (half + half * jnp.tanh(half)).astype(jnp.bfloat16)


def norm_call(blocks, affine, slices):
    units, chan = blocks.shape[0], len(slices)
    return pl.pallas_call(
        functools.partial(norm_kernel, units, chan),
        out_shape=jax.ShapeDtypeStruct((units,) + slices[0].shape[1:], jnp.bfloat16),
        in_specs=[pl.BlockSpec(memory_space=pltpu.SMEM)] + [WHOLE] * (1 + chan),
        out_specs=WHOLE,
        compiler_params=pltpu.CompilerParams(vmem_limit_bytes=VMEM_BYTES),
        cost_estimate=weight(0),
        name="norm_units",
    )(jnp.asarray(blocks.reshape(-1)), affine, *slices)


def conv_kernel(parts, ready, ahead, first, extra, last, *refs):
    refs = list(refs)
    count = len(parts)
    total_ref = None if first else refs.pop(0)
    normed_ref = refs.pop(0)
    weight_refs = [refs.pop(0) for _ in range(count)]
    ready_refs = {unit: refs.pop(0) for unit in ready}
    skip_ref, table_ref = (refs.pop(0), refs.pop(0)) if extra else (None, None)
    out_ref, token_ref = refs.pop(0), refs.pop(0)
    ahead_refs = {unit: refs.pop(0) for unit in ahead}
    even, odd, rounded, sem = refs
    stacks = (even, odd)
    rows = normed_ref.shape[1]
    outs = out_ref.shape[0]
    column = lax.broadcasted_iota(jnp.int32, (1, CELLS), 1) % WIDTH
    inside = [(column > 0).astype(jnp.bfloat16), None, (column < WIDTH - 1).astype(jnp.bfloat16)]
    token_ref[...] = jnp.zeros_like(token_ref)

    def fill(window, unit, taps):
        normed = normed_ref[unit]
        for dx in range(3):
            moved = normed if dx == 1 else shifted(normed, dx - 1) * inside[dx]
            for dy in taps:
                row = (3 * (dy - taps[0]) + dx) * rows
                window[row : row + rows, :] = moved if dy == 1 else shifted(moved, WIDTH * (dy - 1))

    def build(u):
        if parts[u][0] not in ready_refs:
            fill(stacks[u % 2], *parts[u])

    def product(u, here):
        unit, taps = parts[u]
        depth = 3 * len(taps) * rows
        window, row = (ready_refs[unit], 3 * taps[0] * rows) if unit in ready_refs else (stacks[u % 2], 0)
        weights = weight_refs[u][:, :, here].reshape(depth, here.stop - here.start)
        return lax.dot_general(
            weights, window[row : row + depth, :], (((0,), (0,)), ((), ())), preferred_element_type=jnp.float32
        )

    build(0)
    if not last:
        for u in range(count):
            if u + 1 < count:
                build(u + 1)
            else:
                for unit in ahead:
                    fill(ahead_refs[unit], unit, tuple(range(3)))
            part = product(u, slice(0, outs))
            if u == 0 and extra:
                bias = jnp.broadcast_to(table_ref[3:4, :], (128, outs)).T[:, 0:1]
                part = part + (skip_ref[...].astype(jnp.float32) + bias)
            if not (u == 0 and first):
                part = part + (total_ref if u == 0 else out_ref)[...]
            out_ref[...] = part
        return
    tile = 128 if outs % 128 == 0 else outs
    copies = []
    for start in range(0, outs, tile):
        here = slice(start, start + tile)
        rounded[here, :] = (total_ref[here, :] + product(0, here)).astype(jnp.bfloat16)
        part = pl.ds(start, tile)
        copies.append(pltpu.make_async_copy(rounded.at[part], out_ref.at[part], sem.at[start // tile]))
        copies[-1].start()
    for copy in copies:
        copy.wait()


def conv_call(parts, total, normed, weights, extra=(), last=False, ready=None, ahead=()):
    first = total is None
    ready = {unit: window for unit, window in (ready or {}).items() if unit in [p[0] for p in parts]}
    _, rows, _ = normed.shape
    outs = weights[0].shape[2]
    tiles = outs // 128 if outs % 128 == 0 else 1
    operands = ([] if first else [total]) + [normed] + list(weights) + list(ready.values()) + list(extra)
    return pl.pallas_call(
        functools.partial(conv_kernel, tuple(parts), tuple(ready), tuple(ahead), first, bool(extra), last),
        out_shape=[
            jax.ShapeDtypeStruct((outs, CELLS), jnp.bfloat16 if last else jnp.float32),
            jax.ShapeDtypeStruct((8, 128), jnp.float32),
        ]
        + [jax.ShapeDtypeStruct((9 * rows, CELLS), jnp.bfloat16)] * len(ahead),
        in_specs=[WHOLE] * len(operands),
        out_specs=[ANY if last else WHOLE, WHOLE] + [WHOLE] * len(ahead),
        scratch_shapes=[
            pltpu.VMEM((9 * rows, CELLS), jnp.bfloat16),
            pltpu.VMEM((9 * rows, CELLS), jnp.bfloat16),
            pltpu.VMEM((outs, CELLS) if last else (16, 128), jnp.bfloat16),
            pltpu.SemaphoreType.DMA((tiles,)),
        ],
        input_output_aliases={} if first or last else {0: 0},
        compiler_params=pltpu.CompilerParams(vmem_limit_bytes=VMEM_BYTES),
        name="conv_units",
    )(*operands)


def make_body(dp, chan):
    ring = Ring(dp)
    chan_pairs = [(i, (i + 1) % chan) for i in range(chan)]

    def around(value):
        values = [value]
        for _ in range(chan - 1):
            values.append(lax.ppermute(values[-1], "chan", chan_pairs))
        return values

    def body(h_in, skip, emb, w_emb, b_emb, gn_gain, gn_bias, w_conv, b_conv):
        panel = h_in.shape[1]
        rows, outs = w_conv.shape[1], w_conv.shape[2]
        blocks = panel // rows

        own = w_conv.reshape(3, 3 * rows, outs)
        final = len(ring.hops) + 1
        pieces = {0: own, 1: lax.ppermute(own, "dp", ring.core_pairs)}
        pieces[2] = lax.ppermute(own, "dp", ring.pairs)

        slices = around(h_in.reshape(blocks, rows, CELLS))

        def hop(i, *after):
            if after:
                pieces[i - 2] = gate(pieces[i - 2], *after)
            pieces[i] = lax.ppermute(pieces[i - 2], "dp", ring.pairs)

        act = act_call(emb, dp, pieces[1])
        act_rows = lax.all_to_all(act, "dp", 0, 0, tiled=True)
        params = jnp.concatenate([b_emb, gn_gain, gn_bias, b_conv]).reshape(4, panel)
        table = stats_call(h_in[0], params)
        if final >= 3:
            hop(3, act)
        terms = emb_call(act_rows, w_emb)
        if final >= 4:
            hop(4, terms)
        terms = lax.all_to_all(terms, "dp", 0, 0, tiled=True)
        affine = affine_call(C // GROUPS, rows, terms, table, pieces[min(3, final)])
        affine = jnp.concatenate(around(affine), axis=0)
        if final >= 5:
            hop(5)

        normed = norm_call(ring.blocks, affine, slices)

        taps = tuple(range(3))
        units = [((0, taps), own), ((1, taps), pieces[1])]
        tokens = []

        def swapped(piece):
            return lax.ppermute(piece, "dp", ring.core_pairs)

        def arrived(i):
            units.append(((2 * i - 2, taps), pieces[i]))

        def swap(i):
            units.append(((2 * i - 1, taps), swapped(pieces[i])))

        windows = {}

        def convolve(total, count, extra=(), last=False, ahead=()):
            here = [units.pop(0) for _ in range(min(count, len(units)))]
            total, token, *made = conv_call(
                [p for p, _ in here], total, normed, [w for _, w in here], extra, last, windows, ahead
            )
            tokens.append(token)
            windows.update(zip(ahead, made))
            return total

        total = None
        for i in range(2, min(final, 3) + 1):
            arrived(i)
            swap(i)
        if final >= 4:
            total = convolve(total, 4)
        for i in range(6, final + 1):
            after = ([normed] + tokens)[i - 6]
            if i < final:
                hop(i, after)
            else:
                pieces[i - 2] = gate(pieces[i - 2], after)
                tail = [
                    (rows_of_taps, lax.ppermute(pieces[i - 2][rows_of_taps[0] : rows_of_taps[-1] + 1], "dp", ring.pairs))
                    for rows_of_taps in (taps[:2], taps[2:])
                ]
            arrived(i - 2)
            total = convolve(total, 4)
            swap(i - 2)
        if final >= 6:
            pieces[final - 1] = gate(pieces[final - 1], tokens[-1])
            arrived(final - 1)
        else:
            tail = []
            for i in range(4, final + 1):
                arrived(i)
                swap(i)
        while len(units) > 4:
            total = convolve(total, 4)
        extra = (skip[0], table)
        if tail:
            total = convolve(total, len(units), extra, ahead=(2 * final - 2, 2 * final - 1))
            extra = ()
            swap(final - 1)
        for rows_of_taps, piece in tail:
            piece = gate(piece, tokens[-1], times=1)
            units.append(((2 * final - 2, rows_of_taps), piece))
            moving = ((2 * final - 1, rows_of_taps), swapped(piece))
            total = convolve(total, len(units))
            units.append(moving)
        while len(units) > 1:
            total = convolve(total, min(4, len(units) - 1), extra)
            extra = ()
        total = convolve(total, 1, extra, last=True)
        return total[None]

    return body


def solution(mesh):
    return jax.shard_map(
        make_body(mesh.shape["dp"], mesh.shape["chan"]),
        mesh=mesh,
        in_specs=(
            P("dp", "chan", None),
            P("dp", "chan", None),
            P("dp", None),
            P("dp", "chan"),
            P("chan"),
            P("chan"),
            P("chan"),
            P(None, "dp", "chan"),
            P("chan"),
        ),
        out_specs=P("dp", "chan", None),
        check_vma=False,
    )
```

```python
import functools

import jax
import jax.numpy as jnp
import numpy as np
from jax import lax
from jax.experimental import pallas as pl
from jax.experimental.pallas import tpu as pltpu
from jax.sharding import PartitionSpec as P

C = 1280
GROUPS = 32
HEIGHT = 32
WIDTH = 32
CELLS = HEIGHT * WIDTH
VMEM_BYTES = 28 * 2**20
ANY = pl.BlockSpec(memory_space=pl.ANY)
WHOLE = pl.BlockSpec(memory_space=pltpu.VMEM)


def chip_order(chips):
    if chips % 2:
        return list(range(chips))
    half = chips // 2
    return [2 * z for z in range(half)] + [2 * z + 1 for z in reversed(range(half))]


class Ring:
    def __init__(self, dp):
        self.dp = dp
        n = dp // 2
        order = chip_order(n)
        self.core_pairs = [(i, i ^ 1) for i in range(dp)]
        self.pairs = [(2 * order[k], 2 * order[(k + 1) % n]) for k in range(n)]
        self.pairs += [(2 * order[k] + 1, 2 * order[(k - 1) % n] + 1) for k in range(n)]
        full = (n - 1) // 2
        self.hops = [(s, h) for s in range(1, full + 1) for h in range(2)]
        if n % 2 == 0:
            self.hops.append((full + 1, 0))
        self.blocks = np.zeros((dp, dp), np.int32)
        for k in range(n):
            for core in range(2):
                me = 2 * order[k] + core
                units = [me, me ^ 1]
                for s, h in self.hops:
                    for c in (core, 1 - core):
                        chip = order[(k - s) % n] if c == 0 else order[(k + s) % n]
                        units.append(2 * chip + (c if h == 0 else 1 - c))
                self.blocks[me] = units


def weight(times):
    return pl.CostEstimate(flops=int(times * 1e9), transcendentals=0, bytes_accessed=int(times * 4e6))


def nothing(*refs):
    del refs


def gate(piece, *others, times=None):
    return pl.pallas_call(
        nothing,
        out_shape=jax.ShapeDtypeStruct(piece.shape, piece.dtype),
        in_specs=[ANY] * (1 + len(others)),
        out_specs=ANY,
        input_output_aliases={0: 0},
        compiler_params=pltpu.CompilerParams(vmem_limit_bytes=2**20),
        cost_estimate=None if times is None else weight(times),
        name="gate",
    )(piece, *others)


def act_kernel(emb_ref, *refs):
    out_ref = refs[-1]
    v = emb_ref[...].astype(jnp.float32)
    act = (v / (1.0 + jnp.exp(-v))).astype(jnp.bfloat16)
    rows = out_ref.shape[2]
    for d in range(out_ref.shape[0]):
        out_ref[d] = act[:, d * rows : (d + 1) * rows]


def act_call(emb, count, *after):
    return pl.pallas_call(
        act_kernel,
        out_shape=jax.ShapeDtypeStruct((count, 1, emb.shape[1] // count), jnp.bfloat16),
        in_specs=[WHOLE] + [ANY] * len(after),
        out_specs=WHOLE,
        compiler_params=pltpu.CompilerParams(vmem_limit_bytes=VMEM_BYTES),
        name="act_rows",
    )(emb, *after)


def emb_kernel(act_ref, w_ref, out_ref):
    out_ref[:, 0, :] = jnp.dot(act_ref[:, 0, :], w_ref[...], preferred_element_type=jnp.float32)


def emb_call(act_rows, w_emb):
    return pl.pallas_call(
        emb_kernel,
        out_shape=jax.ShapeDtypeStruct((act_rows.shape[0], 1, w_emb.shape[1]), jnp.float32),
        in_specs=[WHOLE, WHOLE],
        out_specs=WHOLE,
        compiler_params=pltpu.CompilerParams(vmem_limit_bytes=VMEM_BYTES),
        name="emb_terms",
    )(act_rows, w_emb)


def stats_kernel(h_ref, params_ref, out_ref):
    panel = h_ref.shape[0]
    step = 80 if panel % 80 == 0 else panel
    count = params_ref.shape[0]
    out_ref[0:count, :] = params_ref[...]
    means, variances = [], []
    for start in range(0, panel, step):
        values = h_ref[start : start + step, :].astype(jnp.float32)
        mean = jnp.mean(values, axis=1, keepdims=True)
        means.append(mean)
        variances.append(jnp.mean((values - mean) ** 2, axis=1, keepdims=True))
    for i, columns in ((count, means), (count + 1, variances)):
        column = jnp.concatenate(columns, axis=0)
        out_ref[i : i + 1, :] = jnp.broadcast_to(column, (panel, 128)).T[0:1, :]


def stats_call(h, params):
    return pl.pallas_call(
        stats_kernel,
        out_shape=jax.ShapeDtypeStruct((params.shape[0] + 2, h.shape[0]), jnp.float32),
        in_specs=[WHOLE, WHOLE],
        out_specs=WHOLE,
        compiler_params=pltpu.CompilerParams(vmem_limit_bytes=VMEM_BYTES),
        cost_estimate=weight(10),
        name="channel_stats",
    )(h, params)


def affine_kernel(size, terms_ref, table_ref, *refs):
    out_ref = refs[-1]
    rows = out_ref.shape[2]
    b_emb, gain, bias, _, channel_mean, channel_var = (table_ref[i : i + 1, :] for i in range(6))
    shift = jnp.sum(terms_ref[...], axis=0) + b_emb
    width = shift.shape[1]
    group = lax.broadcasted_iota(jnp.int32, (width, width // size), 0) // size
    member = (group == lax.broadcasted_iota(jnp.int32, group.shape, 1)).astype(jnp.float32)

    def per_group(row):
        row = jnp.broadcast_to(row, (8, row.shape[1]))
        return jnp.dot(row, member, precision=lax.Precision.HIGHEST, preferred_element_type=jnp.float32) / size

    def per_channel(groups):
        back = (((1,), (1,)), ((), ()))
        spread = lax.dot_general(
            groups, member, back, precision=lax.Precision.HIGHEST, preferred_element_type=jnp.float32
        )
        return spread[0:1, :]

    center = channel_mean + shift
    mean = per_channel(per_group(center))
    var = per_group(channel_var + (center - mean) ** 2)
    scale = per_channel(lax.rsqrt(var + 1e-05)) * gain
    offset = (shift - mean) * scale + bias
    both = jnp.concatenate([scale, offset], axis=0)
    for d in range(out_ref.shape[0]):
        out_ref[d] = both[:, d * rows : (d + 1) * rows]


def affine_call(size, rows, terms, table, *after):
    channels = terms.shape[2]
    return pl.pallas_call(
        functools.partial(affine_kernel, size),
        out_shape=jax.ShapeDtypeStruct((channels // rows, 2, rows), jnp.float32),
        in_specs=[WHOLE, WHOLE] + [ANY] * len(after),
        out_specs=WHOLE,
        compiler_params=pltpu.CompilerParams(vmem_limit_bytes=VMEM_BYTES),
        cost_estimate=weight(7),
        name="affine",
    )(terms, table, *after)


def shifted(values, amount):
    edge = jnp.zeros((values.shape[0], abs(amount)), values.dtype)
    if amount > 0:
        return jnp.concatenate([values[:, amount:], edge], axis=1)
    return jnp.concatenate([edge, values[:, :amount]], axis=1)


def norm_kernel(units, chan, blocks_ref, ab_ref, *refs):
    h_refs, out_ref = refs[:-1], refs[-1]
    blocks = h_refs[0].shape[0]
    me, side = lax.axis_index("dp"), lax.axis_index("chan")
    for u in range(units):
        block = blocks_ref[me * units + u]
        turn, place = lax.rem(side - block // blocks + chan, chan), lax.rem(block, blocks)
        ab = ab_ref[turn * blocks + place].T
        h = h_refs[0][place]
        for other in range(1, chan):
            h = jnp.where(turn == other, h_refs[other][place], h)
        v = h.astype(jnp.float32) * ab[:, 0:1] + ab[:, 1:2]
        half = 0.5 * v
        out_ref[u] = (half + half * jnp.tanh(half)).astype(jnp.bfloat16)


def norm_call(blocks, affine, slices):
    units, chan = blocks.shape[0], len(slices)
    return pl.pallas_call(
        functools.partial(norm_kernel, units, chan),
        out_shape=jax.ShapeDtypeStruct((units,) + slices[0].shape[1:], jnp.bfloat16),
        in_specs=[pl.BlockSpec(memory_space=pltpu.SMEM)] + [WHOLE] * (1 + chan),
        out_specs=WHOLE,
        compiler_params=pltpu.CompilerParams(vmem_limit_bytes=VMEM_BYTES),
        cost_estimate=weight(0),
        name="norm_units",
    )(jnp.asarray(blocks.reshape(-1)), affine, *slices)


def conv_kernel(parts, ready, ahead, first, extra, last, *refs):
    refs = list(refs)
    count = len(parts)
    total_ref = None if first else refs.pop(0)
    normed_ref = refs.pop(0)
    weight_refs = [refs.pop(0) for _ in range(count)]
    ready_refs = {unit: refs.pop(0) for unit in ready}
    skip_ref, table_ref = (refs.pop(0), refs.pop(0)) if extra else (None, None)
    out_ref, token_ref = refs.pop(0), refs.pop(0)
    ahead_refs = {unit: refs.pop(0) for unit in ahead}
    even, odd, rounded, sem = refs
    stacks = (even, odd)
    rows = normed_ref.shape[1]
    outs = out_ref.shape[0]
    column = lax.broadcasted_iota(jnp.int32, (1, CELLS), 1) % WIDTH
    inside = [(column > 0).astype(jnp.bfloat16), None, (column < WIDTH - 1).astype(jnp.bfloat16)]
    token_ref[...] = jnp.zeros_like(token_ref)

    def fill(window, unit, taps):
        normed = normed_ref[unit]
        for dx in range(3):
            moved = normed if dx == 1 else shifted(normed, dx - 1) * inside[dx]
            for dy in taps:
                row = (3 * (dy - taps[0]) + dx) * rows
                window[row : row + rows, :] = moved if dy == 1 else shifted(moved, WIDTH * (dy - 1))

    def build(u):
        if parts[u][0] not in ready_refs:
            fill(stacks[u % 2], *parts[u])

    def product(u, here):
        unit, taps = parts[u]
        depth = 3 * len(taps) * rows
        window, row = (ready_refs[unit], 3 * taps[0] * rows) if unit in ready_refs else (stacks[u % 2], 0)
        weights = weight_refs[u][:, :, here].reshape(depth, here.stop - here.start)
        return lax.dot_general(
            weights, window[row : row + depth, :], (((0,), (0,)), ((), ())), preferred_element_type=jnp.float32
        )

    for u in range(count if last else 1):
        build(u)
    if not last:
        for u in range(count):
            if u + 1 < count:
                build(u + 1)
            else:
                for unit in ahead:
                    fill(ahead_refs[unit], unit, tuple(range(3)))
            part = product(u, slice(0, outs))
            if u == 0 and extra:
                bias = jnp.broadcast_to(table_ref[3:4, :], (128, outs)).T[:, 0:1]
                part = part + (skip_ref[...].astype(jnp.float32) + bias)
            if not (u == 0 and first):
                part = part + (total_ref if u == 0 else out_ref)[...]
            out_ref[...] = part
        return
    tile = 128 if outs % 128 == 0 else outs
    copies = []
    for start in range(0, outs, tile):
        here = slice(start, start + tile)
        value = total_ref[here, :] + product(0, here)
        for u in range(1, count):
            value = value + product(u, here)
        rounded[here, :] = value.astype(jnp.bfloat16)
        part = pl.ds(start, tile)
        copies.append(pltpu.make_async_copy(rounded.at[part], out_ref.at[part], sem.at[start // tile]))
        copies[-1].start()
    for copy in copies:
        copy.wait()


def conv_call(parts, total, normed, weights, extra=(), last=False, ready=None, ahead=()):
    first = total is None
    ready = {unit: window for unit, window in (ready or {}).items() if unit in [p[0] for p in parts]}
    _, rows, _ = normed.shape
    outs = weights[0].shape[2]
    tiles = outs // 128 if outs % 128 == 0 else 1
    operands = ([] if first else [total]) + [normed] + list(weights) + list(ready.values()) + list(extra)
    return pl.pallas_call(
        functools.partial(conv_kernel, tuple(parts), tuple(ready), tuple(ahead), first, bool(extra), last),
        out_shape=[
            jax.ShapeDtypeStruct((outs, CELLS), jnp.bfloat16 if last else jnp.float32),
            jax.ShapeDtypeStruct((8, 128), jnp.float32),
        ]
        + [jax.ShapeDtypeStruct((9 * rows, CELLS), jnp.bfloat16)] * len(ahead),
        in_specs=[WHOLE] * len(operands),
        out_specs=[ANY if last else WHOLE, WHOLE] + [WHOLE] * len(ahead),
        scratch_shapes=[
            pltpu.VMEM((9 * rows, CELLS), jnp.bfloat16),
            pltpu.VMEM((9 * rows, CELLS), jnp.bfloat16),
            pltpu.VMEM((outs, CELLS) if last else (16, 128), jnp.bfloat16),
            pltpu.SemaphoreType.DMA((tiles,)),
        ],
        input_output_aliases={} if first or last else {0: 0},
        compiler_params=pltpu.CompilerParams(vmem_limit_bytes=VMEM_BYTES),
        name="conv_units",
    )(*operands)


def make_body(dp, chan):
    ring = Ring(dp)
    chan_pairs = [(i, (i + 1) % chan) for i in range(chan)]

    def around(value):
        values = [value]
        for _ in range(chan - 1):
            values.append(lax.ppermute(values[-1], "chan", chan_pairs))
        return values

    def body(h_in, skip, emb, w_emb, b_emb, gn_gain, gn_bias, w_conv, b_conv):
        panel = h_in.shape[1]
        rows, outs = w_conv.shape[1], w_conv.shape[2]
        blocks = panel // rows

        own = w_conv.reshape(3, 3 * rows, outs)
        final = len(ring.hops) + 1
        pieces = {0: own, 1: lax.ppermute(own, "dp", ring.core_pairs)}
        pieces[2] = lax.ppermute(own, "dp", ring.pairs)

        slices = around(h_in.reshape(blocks, rows, CELLS))

        def hop(i, *after):
            if after:
                pieces[i - 2] = gate(pieces[i - 2], *after)
            pieces[i] = lax.ppermute(pieces[i - 2], "dp", ring.pairs)

        act = act_call(emb, dp, pieces[1])
        act_rows = lax.all_to_all(act, "dp", 0, 0, tiled=True)
        params = jnp.concatenate([b_emb, gn_gain, gn_bias, b_conv]).reshape(4, panel)
        table = stats_call(h_in[0], params)
        if final >= 3:
            hop(3, act)
        terms = emb_call(act_rows, w_emb)
        if final >= 4:
            hop(4, terms)
        terms = lax.all_to_all(terms, "dp", 0, 0, tiled=True)
        affine = affine_call(C // GROUPS, rows, terms, table, pieces[min(3, final)])
        affine = jnp.concatenate(around(affine), axis=0)
        if final >= 5:
            hop(5)

        normed = norm_call(ring.blocks, affine, slices)

        taps = tuple(range(3))
        units = [((0, taps), own), ((1, taps), pieces[1])]
        tokens = []

        def swapped(piece):
            return lax.ppermute(piece, "dp", ring.core_pairs)

        def arrived(i):
            units.append(((2 * i - 2, taps), pieces[i]))

        def swap(i):
            units.append(((2 * i - 1, taps), swapped(pieces[i])))

        windows = {}

        def convolve(total, count, extra=(), last=False, ahead=()):
            here = [units.pop(0) for _ in range(min(count, len(units)))]
            total, token, *made = conv_call(
                [p for p, _ in here], total, normed, [w for _, w in here], extra, last, windows, ahead
            )
            tokens.append(token)
            windows.update(zip(ahead, made))
            return total

        total = None
        for i in range(2, min(final, 3) + 1):
            arrived(i)
            swap(i)
        if final >= 4:
            total = convolve(total, 4)
        for i in range(6, final + 1):
            after = ([normed] + tokens)[i - 6]
            if i < final:
                hop(i, after)
            else:
                pieces[i - 2] = gate(pieces[i - 2], after)
                tail = [
                    (rows_of_taps, lax.ppermute(pieces[i - 2][rows_of_taps[0] : rows_of_taps[-1] + 1], "dp", ring.pairs))
                    for rows_of_taps in (taps[:2], taps[2:])
                ]
            arrived(i - 2)
            total = convolve(total, 4)
            swap(i - 2)
        if final >= 6:
            pieces[final - 1] = gate(pieces[final - 1], tokens[-1])
            arrived(final - 1)
        else:
            tail = []
            for i in range(4, final + 1):
                arrived(i)
                swap(i)
        while len(units) > 4:
            total = convolve(total, 4)
        extra = (skip[0], table)
        if tail:
            total = convolve(total, len(units), extra, ahead=(2 * final - 2, 2 * final - 1))
            extra = ()
            swap(final - 1)
        for rows_of_taps, piece in tail:
            piece = gate(piece, tokens[-1], times=1)
            if rows_of_taps == tail[0][0]:
                units.append(((2 * final - 2, rows_of_taps), piece))
            total = convolve(total, len(units))
            if rows_of_taps != tail[0][0]:
                units.append(((2 * final - 2, rows_of_taps), piece))
            units.append(((2 * final - 1, rows_of_taps), swapped(piece)))
        while len(units) > 2:
            total = convolve(total, min(4, len(units) - 2), extra)
            extra = ()
        total = convolve(total, len(units), extra, last=True)
        return total[None]

    return body


def solution(mesh):
    return jax.shard_map(
        make_body(mesh.shape["dp"], mesh.shape["chan"]),
        mesh=mesh,
        in_specs=(
            P("dp", "chan", None),
            P("dp", "chan", None),
            P("dp", None),
            P("dp", "chan"),
            P("chan"),
            P("chan"),
            P("chan"),
            P(None, "dp", "chan"),
            P("chan"),
        ),
        out_specs=P("dp", "chan", None),
        check_vma=False,
    )
```

```python
import functools

import jax
import jax.numpy as jnp
import numpy as np
from jax import lax
from jax.experimental import pallas as pl
from jax.experimental.pallas import tpu as pltpu
from jax.sharding import PartitionSpec as P

C = 1280
GROUPS = 32
HEIGHT = 32
WIDTH = 32
CELLS = HEIGHT * WIDTH
VMEM_BYTES = 28 * 2**20
ANY = pl.BlockSpec(memory_space=pl.ANY)
WHOLE = pl.BlockSpec(memory_space=pltpu.VMEM)


def chip_order(chips):
    if chips % 2:
        return list(range(chips))
    half = chips // 2
    return [2 * z for z in range(half)] + [2 * z + 1 for z in reversed(range(half))]


class Ring:
    def __init__(self, dp):
        self.dp = dp
        n = dp // 2
        order = chip_order(n)
        self.core_pairs = [(i, i ^ 1) for i in range(dp)]
        self.pairs = [(2 * order[k], 2 * order[(k + 1) % n]) for k in range(n)]
        self.pairs += [(2 * order[k] + 1, 2 * order[(k - 1) % n] + 1) for k in range(n)]
        full = (n - 1) // 2
        self.hops = [(s, h) for s in range(1, full + 1) for h in range(2)]
        if n % 2 == 0:
            self.hops.append((full + 1, 0))
        self.blocks = np.zeros((dp, dp), np.int32)
        for k in range(n):
            for core in range(2):
                me = 2 * order[k] + core
                units = [me, me ^ 1]
                for s, h in self.hops:
                    for c in (core, 1 - core):
                        chip = order[(k - s) % n] if c == 0 else order[(k + s) % n]
                        units.append(2 * chip + (c if h == 0 else 1 - c))
                self.blocks[me] = units


def weight(times):
    return pl.CostEstimate(flops=int(times * 1e9), transcendentals=0, bytes_accessed=int(times * 4e6))


def nothing(*refs):
    del refs


def gate(piece, *others, times=None):
    return pl.pallas_call(
        nothing,
        out_shape=jax.ShapeDtypeStruct(piece.shape, piece.dtype),
        in_specs=[ANY] * (1 + len(others)),
        out_specs=ANY,
        input_output_aliases={0: 0},
        compiler_params=pltpu.CompilerParams(vmem_limit_bytes=2**20),
        cost_estimate=None if times is None else weight(times),
        name="gate",
    )(piece, *others)


def act_kernel(emb_ref, *refs):
    out_ref = refs[-1]
    v = emb_ref[...].astype(jnp.float32)
    act = (v / (1.0 + jnp.exp(-v))).astype(jnp.bfloat16)
    rows = out_ref.shape[2]
    for d in range(out_ref.shape[0]):
        out_ref[d] = act[:, d * rows : (d + 1) * rows]


def act_call(emb, count, *after):
    return pl.pallas_call(
        act_kernel,
        out_shape=jax.ShapeDtypeStruct((count, 1, emb.shape[1] // count), jnp.bfloat16),
        in_specs=[WHOLE] + [ANY] * len(after),
        out_specs=WHOLE,
        compiler_params=pltpu.CompilerParams(vmem_limit_bytes=VMEM_BYTES),
        name="act_rows",
    )(emb, *after)


def emb_kernel(act_ref, w_ref, out_ref):
    out_ref[:, 0, :] = jnp.dot(act_ref[:, 0, :], w_ref[...], preferred_element_type=jnp.float32)


def emb_call(act_rows, w_emb):
    return pl.pallas_call(
        emb_kernel,
        out_shape=jax.ShapeDtypeStruct((act_rows.shape[0], 1, w_emb.shape[1]), jnp.float32),
        in_specs=[WHOLE, WHOLE],
        out_specs=WHOLE,
        compiler_params=pltpu.CompilerParams(vmem_limit_bytes=VMEM_BYTES),
        name="emb_terms",
    )(act_rows, w_emb)


def stats_kernel(h_ref, *refs):
    panel = h_ref.shape[0]
    step = 80 if panel % 80 == 0 else panel
    params, out_ref = refs[:-1], refs[-1]
    count = len(params)
    for i in range(count):
        out_ref[i : i + 1, :] = params[i][...].reshape(1, panel)
    means, variances = [], []
    for start in range(0, panel, step):
        values = h_ref[start : start + step, :].astype(jnp.float32)
        mean = jnp.mean(values, axis=1, keepdims=True)
        means.append(mean)
        variances.append(jnp.mean((values - mean) ** 2, axis=1, keepdims=True))
    for i, columns in ((count, means), (count + 1, variances)):
        column = jnp.concatenate(columns, axis=0)
        out_ref[i : i + 1, :] = jnp.broadcast_to(column, (panel, 128)).T[0:1, :]


def stats_call(h, *params):
    return pl.pallas_call(
        stats_kernel,
        out_shape=jax.ShapeDtypeStruct((len(params) + 2, h.shape[0]), jnp.float32),
        in_specs=[WHOLE] * (1 + len(params)),
        out_specs=WHOLE,
        compiler_params=pltpu.CompilerParams(vmem_limit_bytes=VMEM_BYTES),
        cost_estimate=weight(10),
        name="channel_stats",
    )(h, *params)


def affine_kernel(size, terms_ref, table_ref, *refs):
    out_ref = refs[-1]
    rows = out_ref.shape[2]
    b_emb, gain, bias, _, channel_mean, channel_var = (table_ref[i : i + 1, :] for i in range(6))
    shift = jnp.sum(terms_ref[...], axis=0) + b_emb
    width = shift.shape[1]
    group = lax.broadcasted_iota(jnp.int32, (width, width // size), 0) // size
    member = (group == lax.broadcasted_iota(jnp.int32, group.shape, 1)).astype(jnp.float32)

    def per_group(row):
        row = jnp.broadcast_to(row, (8, row.shape[1]))
        return jnp.dot(row, member, precision=lax.Precision.HIGHEST, preferred_element_type=jnp.float32) / size

    def per_channel(groups):
        back = (((1,), (1,)), ((), ()))
        spread = lax.dot_general(
            groups, member, back, precision=lax.Precision.HIGHEST, preferred_element_type=jnp.float32
        )
        return spread[0:1, :]

    center = channel_mean + shift
    mean = per_channel(per_group(center))
    var = per_group(channel_var + (center - mean) ** 2)
    scale = per_channel(lax.rsqrt(var + 1e-05)) * gain
    offset = (shift - mean) * scale + bias
    both = jnp.concatenate([scale, offset], axis=0)
    for d in range(out_ref.shape[0]):
        out_ref[d] = both[:, d * rows : (d + 1) * rows]


def affine_call(size, rows, terms, table, *after):
    channels = terms.shape[2]
    return pl.pallas_call(
        functools.partial(affine_kernel, size),
        out_shape=jax.ShapeDtypeStruct((channels // rows, 2, rows), jnp.float32),
        in_specs=[WHOLE, WHOLE] + [ANY] * len(after),
        out_specs=WHOLE,
        compiler_params=pltpu.CompilerParams(vmem_limit_bytes=VMEM_BYTES),
        cost_estimate=weight(7),
        name="affine",
    )(terms, table, *after)


def shifted(values, amount):
    edge = jnp.zeros((values.shape[0], abs(amount)), values.dtype)
    if amount > 0:
        return jnp.concatenate([values[:, amount:], edge], axis=1)
    return jnp.concatenate([edge, values[:, :amount]], axis=1)


def norm_kernel(units, chan, blocks_ref, ab_ref, *refs):
    h_refs, out_ref = refs[:-1], refs[-1]
    blocks = h_refs[0].shape[0]
    me, side = lax.axis_index("dp"), lax.axis_index("chan")
    for u in range(units):
        block = blocks_ref[me * units + u]
        turn, place = lax.rem(side - block // blocks + chan, chan), lax.rem(block, blocks)
        ab = ab_ref[turn * blocks + place].T
        h = h_refs[0][place]
        for other in range(1, chan):
            h = jnp.where(turn == other, h_refs[other][place], h)
        v = h.astype(jnp.float32) * ab[:, 0:1] + ab[:, 1:2]
        half = 0.5 * v
        out_ref[u] = (half + half * jnp.tanh(half)).astype(jnp.bfloat16)


def norm_call(blocks, affine, slices):
    units, chan = blocks.shape[0], len(slices)
    return pl.pallas_call(
        functools.partial(norm_kernel, units, chan),
        out_shape=jax.ShapeDtypeStruct((units,) + slices[0].shape[1:], jnp.bfloat16),
        in_specs=[pl.BlockSpec(memory_space=pltpu.SMEM)] + [WHOLE] * (1 + chan),
        out_specs=WHOLE,
        compiler_params=pltpu.CompilerParams(vmem_limit_bytes=VMEM_BYTES),
        cost_estimate=weight(0),
        name="norm_units",
    )(jnp.asarray(blocks.reshape(-1)), affine, *slices)


def conv_kernel(parts, ready, ahead, first, extra, last, *refs):
    refs = list(refs)
    count = len(parts)
    total_ref = None if first else refs.pop(0)
    normed_ref = refs.pop(0)
    weight_refs = [refs.pop(0) for _ in range(count)]
    ready_refs = {unit: refs.pop(0) for unit in ready}
    skip_ref, table_ref = (refs.pop(0), refs.pop(0)) if extra else (None, None)
    out_ref, token_ref = refs.pop(0), refs.pop(0)
    ahead_refs = {unit: refs.pop(0) for unit in ahead}
    even, odd, rounded, sem = refs
    stacks = (even, odd)
    rows = normed_ref.shape[1]
    outs = out_ref.shape[0]
    column = lax.broadcasted_iota(jnp.int32, (1, CELLS), 1) % WIDTH
    inside = [(column > 0).astype(jnp.bfloat16), None, (column < WIDTH - 1).astype(jnp.bfloat16)]
    token_ref[...] = jnp.zeros_like(token_ref)

    def fill(window, unit, taps):
        normed = normed_ref[unit]
        for dx in range(3):
            moved = normed if dx == 1 else shifted(normed, dx - 1) * inside[dx]
            for dy in taps:
                row = (3 * (dy - taps[0]) + dx) * rows
                window[row : row + rows, :] = moved if dy == 1 else shifted(moved, WIDTH * (dy - 1))

    def build(u):
        if parts[u][0] not in ready_refs:
            fill(stacks[u % 2], *parts[u])

    def product(u, here):
        unit, taps = parts[u]
        depth = 3 * len(taps) * rows
        window, row = (ready_refs[unit], 3 * taps[0] * rows) if unit in ready_refs else (stacks[u % 2], 0)
        weights = weight_refs[u][:, :, here].reshape(depth, here.stop - here.start)
        return lax.dot_general(
            weights, window[row : row + depth, :], (((0,), (0,)), ((), ())), preferred_element_type=jnp.float32
        )

    for u in range(count if last else 1):
        build(u)
    if not last:
        for u in range(count):
            if u + 1 < count:
                build(u + 1)
            else:
                for unit in ahead:
                    fill(ahead_refs[unit], unit, tuple(range(3)))
            part = product(u, slice(0, outs))
            if u == 0 and extra:
                bias = jnp.broadcast_to(table_ref[3:4, :], (128, outs)).T[:, 0:1]
                part = part + (skip_ref[...].astype(jnp.float32) + bias)
            if not (u == 0 and first):
                part = part + (total_ref if u == 0 else out_ref)[...]
            out_ref[...] = part
        return
    tile = 128 if outs % 128 == 0 else outs
    copies = []
    for start in range(0, outs, tile):
        here = slice(start, start + tile)
        value = total_ref[here, :] + product(0, here)
        for u in range(1, count):
            value = value + product(u, here)
        rounded[here, :] = value.astype(jnp.bfloat16)
        part = pl.ds(start, tile)
        copies.append(pltpu.make_async_copy(rounded.at[part], out_ref.at[part], sem.at[start // tile]))
        copies[-1].start()
    for copy in copies:
        copy.wait()


def conv_call(parts, total, normed, weights, extra=(), last=False, ready=None, ahead=()):
    first = total is None
    ready = {unit: window for unit, window in (ready or {}).items() if unit in [p[0] for p in parts]}
    _, rows, _ = normed.shape
    outs = weights[0].shape[2]
    tiles = outs // 128 if outs % 128 == 0 else 1
    operands = ([] if first else [total]) + [normed] + list(weights) + list(ready.values()) + list(extra)
    return pl.pallas_call(
        functools.partial(conv_kernel, tuple(parts), tuple(ready), tuple(ahead), first, bool(extra), last),
        out_shape=[
            jax.ShapeDtypeStruct((outs, CELLS), jnp.bfloat16 if last else jnp.float32),
            jax.ShapeDtypeStruct((8, 128), jnp.float32),
        ]
        + [jax.ShapeDtypeStruct((9 * rows, CELLS), jnp.bfloat16)] * len(ahead),
        in_specs=[WHOLE] * len(operands),
        out_specs=[ANY if last else WHOLE, WHOLE] + [WHOLE] * len(ahead),
        scratch_shapes=[
            pltpu.VMEM((9 * rows, CELLS), jnp.bfloat16),
            pltpu.VMEM((9 * rows, CELLS), jnp.bfloat16),
            pltpu.VMEM((outs, CELLS) if last else (16, 128), jnp.bfloat16),
            pltpu.SemaphoreType.DMA((tiles,)),
        ],
        input_output_aliases={} if first or last else {0: 0},
        compiler_params=pltpu.CompilerParams(vmem_limit_bytes=VMEM_BYTES),
        name="conv_units",
    )(*operands)


def make_body(dp, chan):
    ring = Ring(dp)
    chan_pairs = [(i, (i + 1) % chan) for i in range(chan)]

    def around(value):
        values = [value]
        for _ in range(chan - 1):
            values.append(lax.ppermute(values[-1], "chan", chan_pairs))
        return values

    def body(h_in, skip, emb, w_emb, b_emb, gn_gain, gn_bias, w_conv, b_conv):
        panel = h_in.shape[1]
        rows, outs = w_conv.shape[1], w_conv.shape[2]
        blocks = panel // rows

        own = w_conv.reshape(3, 3 * rows, outs)
        final = len(ring.hops) + 1
        pieces = {0: own, 1: lax.ppermute(own, "dp", ring.core_pairs)}
        pieces[2] = lax.ppermute(own, "dp", ring.pairs)

        slices = around(h_in.reshape(blocks, rows, CELLS))

        def hop(i, *after):
            if after:
                pieces[i - 2] = gate(pieces[i - 2], *after, times=3 if i == 3 else None)
            pieces[i] = lax.ppermute(pieces[i - 2], "dp", ring.pairs)

        act = act_call(emb, dp, pieces[1])
        act_rows = lax.all_to_all(act, "dp", 0, 0, tiled=True)
        table = stats_call(h_in[0], b_emb, gn_gain, gn_bias, b_conv)
        if final >= 3:
            hop(3, act)
        terms = emb_call(act_rows, w_emb)
        if final >= 4:
            hop(4, terms)
        terms = lax.all_to_all(terms, "dp", 0, 0, tiled=True)
        affine = affine_call(C // GROUPS, rows, terms, table, pieces[min(3, final)])
        affine = jnp.concatenate(around(affine), axis=0)
        if final >= 5:
            hop(5)

        normed = norm_call(ring.blocks, affine, slices)

        taps = tuple(range(3))
        units = [((0, taps), own), ((1, taps), pieces[1])]
        tokens = []

        def swapped(piece):
            return lax.ppermute(piece, "dp", ring.core_pairs)

        def arrived(i):
            units.append(((2 * i - 2, taps), pieces[i]))

        def swap(i):
            units.append(((2 * i - 1, taps), swapped(pieces[i])))

        windows = {}

        def convolve(total, count, extra=(), last=False, ahead=()):
            here = [units.pop(0) for _ in range(min(count, len(units)))]
            total, token, *made = conv_call(
                [p for p, _ in here], total, normed, [w for _, w in here], extra, last, windows, ahead
            )
            tokens.append(token)
            windows.update(zip(ahead, made))
            return total

        total = None
        for i in range(2, min(final, 3) + 1):
            arrived(i)
            swap(i)
        if final >= 4:
            total = convolve(total, 4)
        for i in range(6, final + 1):
            after = ([normed] + tokens)[i - 6]
            if i < final:
                hop(i, after)
            else:
                pieces[i - 2] = gate(pieces[i - 2], after)
                tail = [
                    (rows_of_taps, lax.ppermute(pieces[i - 2][rows_of_taps[0] : rows_of_taps[-1] + 1], "dp", ring.pairs))
                    for rows_of_taps in (taps[:2], taps[2:])
                ]
            arrived(i - 2)
            total = convolve(total, 4)
            swap(i - 2)
        if final >= 6:
            pieces[final - 1] = gate(pieces[final - 1], tokens[-1])
            arrived(final - 1)
        else:
            tail = []
            for i in range(4, final + 1):
                arrived(i)
                swap(i)
        while len(units) > 4:
            total = convolve(total, 4)
        extra = (skip[0], table)
        if tail:
            total = convolve(total, len(units), extra, ahead=(2 * final - 2, 2 * final - 1))
            extra = ()
            swap(final - 1)
        for rows_of_taps, piece in tail:
            piece = gate(piece, tokens[-1], times=1)
            if rows_of_taps == tail[0][0]:
                units.append(((2 * final - 2, rows_of_taps), piece))
            total = convolve(total, len(units))
            if rows_of_taps != tail[0][0]:
                units.append(((2 * final - 2, rows_of_taps), piece))
            units.append(((2 * final - 1, rows_of_taps), swapped(piece)))
        while len(units) > 2:
            total = convolve(total, min(4, len(units) - 2), extra)
            extra = ()
        total = convolve(total, len(units), extra, last=True)
        return total[None]

    return body


def solution(mesh):
    return jax.shard_map(
        make_body(mesh.shape["dp"], mesh.shape["chan"]),
        mesh=mesh,
        in_specs=(
            P("dp", "chan", None),
            P("dp", "chan", None),
            P("dp", None),
            P("dp", "chan"),
            P("chan"),
            P("chan"),
            P("chan"),
            P(None, "dp", "chan"),
            P("chan"),
        ),
        out_specs=P("dp", "chan", None),
        check_vma=False,
    )
```

```python
import functools

import jax
import jax.numpy as jnp
import numpy as np
from jax import lax
from jax.experimental import pallas as pl
from jax.experimental.pallas import tpu as pltpu
from jax.sharding import PartitionSpec as P

C = 1280
GROUPS = 32
HEIGHT = 32
WIDTH = 32
CELLS = HEIGHT * WIDTH
VMEM_BYTES = 24 * 2**20
ANY = pl.BlockSpec(memory_space=pl.ANY)
WHOLE = pl.BlockSpec(memory_space=pltpu.VMEM)


def chip_order(chips):
    if chips % 2:
        return list(range(chips))
    half = chips // 2
    return [2 * z for z in range(half)] + [2 * z + 1 for z in reversed(range(half))]


class Ring:
    def __init__(self, dp):
        self.dp = dp
        n = dp // 2
        order = chip_order(n)
        self.core_pairs = [(i, i ^ 1) for i in range(dp)]
        self.pairs = [(2 * order[k], 2 * order[(k + 1) % n]) for k in range(n)]
        self.pairs += [(2 * order[k] + 1, 2 * order[(k - 1) % n] + 1) for k in range(n)]
        full = (n - 1) // 2
        self.hops = [(s, h) for s in range(1, full + 1) for h in range(2)]
        if n % 2 == 0:
            self.hops.append((full + 1, 0))
        self.blocks = np.zeros((dp, dp), np.int32)
        for k in range(n):
            for core in range(2):
                me = 2 * order[k] + core
                units = [me, me ^ 1]
                for s, h in self.hops:
                    for c in (core, 1 - core):
                        chip = order[(k - s) % n] if c == 0 else order[(k + s) % n]
                        units.append(2 * chip + (c if h == 0 else 1 - c))
                self.blocks[me] = units


def weight(times):
    return pl.CostEstimate(flops=int(times * 1e9), transcendentals=0, bytes_accessed=int(times * 4e6))


def nothing(*refs):
    del refs


def gate(piece, *others, times=None):
    return pl.pallas_call(
        nothing,
        out_shape=jax.ShapeDtypeStruct(piece.shape, piece.dtype),
        in_specs=[ANY] * (1 + len(others)),
        out_specs=ANY,
        input_output_aliases={0: 0},
        compiler_params=pltpu.CompilerParams(vmem_limit_bytes=2**20),
        cost_estimate=None if times is None else weight(times),
        name="gate",
    )(piece, *others)


def act_kernel(emb_ref, *refs):
    out_ref = refs[-1]
    v = emb_ref[...].astype(jnp.float32)
    act = (v / (1.0 + jnp.exp(-v))).astype(jnp.bfloat16)
    rows = out_ref.shape[2]
    for d in range(out_ref.shape[0]):
        out_ref[d] = act[:, d * rows : (d + 1) * rows]


def act_call(emb, count, *after):
    return pl.pallas_call(
        act_kernel,
        out_shape=jax.ShapeDtypeStruct((count, 1, emb.shape[1] // count), jnp.bfloat16),
        in_specs=[WHOLE] + [ANY] * len(after),
        out_specs=WHOLE,
        compiler_params=pltpu.CompilerParams(vmem_limit_bytes=VMEM_BYTES),
        name="act_rows",
    )(emb, *after)


def emb_kernel(act_ref, w_ref, out_ref):
    out_ref[:, 0, :] = jnp.dot(act_ref[:, 0, :], w_ref[...], preferred_element_type=jnp.float32)


def emb_call(act_rows, w_emb):
    return pl.pallas_call(
        emb_kernel,
        out_shape=jax.ShapeDtypeStruct((act_rows.shape[0], 1, w_emb.shape[1]), jnp.float32),
        in_specs=[WHOLE, WHOLE],
        out_specs=WHOLE,
        compiler_params=pltpu.CompilerParams(vmem_limit_bytes=VMEM_BYTES),
        name="emb_terms",
    )(act_rows, w_emb)


def stats_kernel(h_ref, *refs):
    panel = h_ref.shape[0]
    step = 80 if panel % 80 == 0 else panel
    params, out_ref = refs[:-1], refs[-1]
    count = len(params)
    for i in range(count):
        out_ref[i : i + 1, :] = params[i][...].reshape(1, panel)
    means, variances = [], []
    for start in range(0, panel, step):
        values = h_ref[start : start + step, :].astype(jnp.float32)
        mean = jnp.mean(values, axis=1, keepdims=True)
        means.append(mean)
        variances.append(jnp.mean((values - mean) ** 2, axis=1, keepdims=True))
    for i, columns in ((count, means), (count + 1, variances)):
        column = jnp.concatenate(columns, axis=0)
        out_ref[i : i + 1, :] = jnp.broadcast_to(column, (panel, 128)).T[0:1, :]


def stats_call(h, *params):
    return pl.pallas_call(
        stats_kernel,
        out_shape=jax.ShapeDtypeStruct((len(params) + 2, h.shape[0]), jnp.float32),
        in_specs=[WHOLE] * (1 + len(params)),
        out_specs=WHOLE,
        compiler_params=pltpu.CompilerParams(vmem_limit_bytes=VMEM_BYTES),
        cost_estimate=weight(10),
        name="channel_stats",
    )(h, *params)


def affine_kernel(size, terms_ref, table_ref, *refs):
    out_ref = refs[-1]
    rows = out_ref.shape[2]
    b_emb, gain, bias, _, channel_mean, channel_var = (table_ref[i : i + 1, :] for i in range(6))
    shift = jnp.sum(terms_ref[...], axis=0) + b_emb
    width = shift.shape[1]
    group = lax.broadcasted_iota(jnp.int32, (width, width // size), 0) // size
    member = (group == lax.broadcasted_iota(jnp.int32, group.shape, 1)).astype(jnp.float32)

    def per_group(row):
        row = jnp.broadcast_to(row, (8, row.shape[1]))
        return jnp.dot(row, member, precision=lax.Precision.HIGHEST, preferred_element_type=jnp.float32) / size

    def per_channel(groups):
        back = (((1,), (1,)), ((), ()))
        spread = lax.dot_general(
            groups, member, back, precision=lax.Precision.HIGHEST, preferred_element_type=jnp.float32
        )
        return spread[0:1, :]

    center = channel_mean + shift
    mean = per_channel(per_group(center))
    var = per_group(channel_var + (center - mean) ** 2)
    scale = per_channel(lax.rsqrt(var + 1e-05)) * gain
    offset = (shift - mean) * scale + bias
    both = jnp.concatenate([scale, offset], axis=0)
    for d in range(out_ref.shape[0]):
        out_ref[d] = both[:, d * rows : (d + 1) * rows]


def affine_call(size, rows, terms, table, *after):
    channels = terms.shape[2]
    return pl.pallas_call(
        functools.partial(affine_kernel, size),
        out_shape=jax.ShapeDtypeStruct((channels // rows, 2, rows), jnp.float32),
        in_specs=[WHOLE, WHOLE] + [ANY] * len(after),
        out_specs=WHOLE,
        compiler_params=pltpu.CompilerParams(vmem_limit_bytes=VMEM_BYTES),
        cost_estimate=weight(7),
        name="affine",
    )(terms, table, *after)


def shifted(values, amount):
    edge = jnp.zeros((values.shape[0], abs(amount)), values.dtype)
    if amount > 0:
        return jnp.concatenate([values[:, amount:], edge], axis=1)
    return jnp.concatenate([edge, values[:, :amount]], axis=1)


def norm_kernel(units, chan, blocks_ref, ab_ref, *refs):
    h_refs, out_ref = refs[:-1], refs[-1]
    blocks = h_refs[0].shape[0]
    me, side = lax.axis_index("dp"), lax.axis_index("chan")
    for u in range(units):
        block = blocks_ref[me * units + u]
        turn, place = lax.rem(side - block // blocks + chan, chan), lax.rem(block, blocks)
        ab = ab_ref[turn * blocks + place].T
        h = h_refs[0][place]
        for other in range(1, chan):
            h = jnp.where(turn == other, h_refs[other][place], h)
        v = h.astype(jnp.float32) * ab[:, 0:1] + ab[:, 1:2]
        half = 0.5 * v
        out_ref[u] = (half + half * jnp.tanh(half)).astype(jnp.bfloat16)


def norm_call(blocks, affine, slices):
    units, chan = blocks.shape[0], len(slices)
    return pl.pallas_call(
        functools.partial(norm_kernel, units, chan),
        out_shape=jax.ShapeDtypeStruct((units,) + slices[0].shape[1:], jnp.bfloat16),
        in_specs=[pl.BlockSpec(memory_space=pltpu.SMEM)] + [WHOLE] * (1 + chan),
        out_specs=WHOLE,
        compiler_params=pltpu.CompilerParams(vmem_limit_bytes=VMEM_BYTES),
        cost_estimate=weight(0),
        name="norm_units",
    )(jnp.asarray(blocks.reshape(-1)), affine, *slices)


def conv_kernel(parts, ready, ahead, first, extra, last, *refs):
    refs = list(refs)
    count = len(parts)
    total_ref = None if first else refs.pop(0)
    normed_ref = refs.pop(0)
    weight_refs = [refs.pop(0) for _ in range(count)]
    ready_refs = {unit: refs.pop(0) for unit in ready}
    skip_ref, table_ref = (refs.pop(0), refs.pop(0)) if extra else (None, None)
    out_ref, token_ref = refs.pop(0), refs.pop(0)
    ahead_refs = {unit: refs.pop(0) for unit in ahead}
    even, odd, rounded, sem = refs
    stacks = (even, odd)
    rows = normed_ref.shape[1]
    outs = out_ref.shape[0]
    column = lax.broadcasted_iota(jnp.int32, (1, CELLS), 1) % WIDTH
    inside = [(column > 0).astype(jnp.bfloat16), None, (column < WIDTH - 1).astype(jnp.bfloat16)]
    token_ref[...] = jnp.zeros_like(token_ref)

    def fill(window, unit, taps):
        normed = normed_ref[unit]
        for dx in range(3):
            moved = normed if dx == 1 else shifted(normed, dx - 1) * inside[dx]
            for dy in taps:
                row = (3 * (dy - taps[0]) + dx) * rows
                window[row : row + rows, :] = moved if dy == 1 else shifted(moved, WIDTH * (dy - 1))

    def build(u):
        if parts[u][0] not in ready_refs:
            fill(stacks[u % 2], *parts[u])

    def product(u, here):
        unit, taps = parts[u]
        depth = 3 * len(taps) * rows
        window, row = (ready_refs[unit], 3 * taps[0] * rows) if unit in ready_refs else (stacks[u % 2], 0)
        weights = weight_refs[u][:, :, here].reshape(depth, here.stop - here.start)
        return lax.dot_general(
            weights, window[row : row + depth, :], (((0,), (0,)), ((), ())), preferred_element_type=jnp.float32
        )

    for u in range(count if last else 1):
        build(u)
    if not last:
        for u in range(count):
            if u + 1 < count:
                build(u + 1)
            else:
                for unit in ahead:
                    fill(ahead_refs[unit], unit, tuple(range(3)))
            part = product(u, slice(0, outs))
            if u == 0 and extra:
                bias = jnp.broadcast_to(table_ref[3:4, :], (128, outs)).T[:, 0:1]
                part = part + (skip_ref[...].astype(jnp.float32) + bias)
            if not (u == 0 and first):
                part = part + (total_ref if u == 0 else out_ref)[...]
            out_ref[...] = part
        return
    tile = 128 if outs % 128 == 0 else outs
    copies = []
    for start in range(0, outs, tile):
        here = slice(start, start + tile)
        value = total_ref[here, :] + product(0, here)
        for u in range(1, count):
            value = value + product(u, here)
        rounded[here, :] = value.astype(jnp.bfloat16)
        part = pl.ds(start, tile)
        copies.append(pltpu.make_async_copy(rounded.at[part], out_ref.at[part], sem.at[start // tile]))
        copies[-1].start()
    for copy in copies:
        copy.wait()


def conv_call(parts, total, normed, weights, extra=(), last=False, ready=None, ahead=()):
    first = total is None
    ready = {unit: window for unit, window in (ready or {}).items() if unit in [p[0] for p in parts]}
    _, rows, _ = normed.shape
    outs = weights[0].shape[2]
    tiles = outs // 128 if outs % 128 == 0 else 1
    operands = ([] if first else [total]) + [normed] + list(weights) + list(ready.values()) + list(extra)
    return pl.pallas_call(
        functools.partial(conv_kernel, tuple(parts), tuple(ready), tuple(ahead), first, bool(extra), last),
        out_shape=[
            jax.ShapeDtypeStruct((outs, CELLS), jnp.bfloat16 if last else jnp.float32),
            jax.ShapeDtypeStruct((8, 128), jnp.float32),
        ]
        + [jax.ShapeDtypeStruct((9 * rows, CELLS), jnp.bfloat16)] * len(ahead),
        in_specs=[WHOLE] * len(operands),
        out_specs=[ANY if last else WHOLE, WHOLE] + [WHOLE] * len(ahead),
        scratch_shapes=[
            pltpu.VMEM((9 * rows, CELLS), jnp.bfloat16),
            pltpu.VMEM((9 * rows, CELLS), jnp.bfloat16),
            pltpu.VMEM((outs, CELLS) if last else (16, 128), jnp.bfloat16),
            pltpu.SemaphoreType.DMA((tiles,)),
        ],
        input_output_aliases={} if first or last else {0: 0},
        compiler_params=pltpu.CompilerParams(vmem_limit_bytes=VMEM_BYTES),
        name="conv_units",
    )(*operands)


def make_body(dp, chan):
    ring = Ring(dp)
    chan_pairs = [(i, (i + 1) % chan) for i in range(chan)]

    def around(value):
        values = [value]
        for _ in range(chan - 1):
            values.append(lax.ppermute(values[-1], "chan", chan_pairs))
        return values

    def body(h_in, skip, emb, w_emb, b_emb, gn_gain, gn_bias, w_conv, b_conv):
        panel = h_in.shape[1]
        rows, outs = w_conv.shape[1], w_conv.shape[2]
        blocks = panel // rows

        own = w_conv.reshape(3, 3 * rows, outs)
        final = len(ring.hops) + 1
        pieces = {0: own, 1: lax.ppermute(own, "dp", ring.core_pairs)}
        pieces[2] = lax.ppermute(own, "dp", ring.pairs)

        slices = around(h_in.reshape(blocks, rows, CELLS))

        def hop(i, *after):
            if after:
                pieces[i - 2] = gate(pieces[i - 2], *after, times=3 if i == 3 else None)
            pieces[i] = lax.ppermute(pieces[i - 2], "dp", ring.pairs)

        act = act_call(emb, dp, pieces[1])
        act_rows = lax.all_to_all(act, "dp", 0, 0, tiled=True)
        table = stats_call(h_in[0], b_emb, gn_gain, gn_bias, b_conv)
        if final >= 3:
            hop(3, act)
        terms = emb_call(act_rows, w_emb)
        if final >= 4:
            hop(4, terms)
        terms = lax.all_to_all(terms, "dp", 0, 0, tiled=True)
        affine = affine_call(C // GROUPS, rows, terms, table, pieces[min(3, final)])
        affine = jnp.concatenate(around(affine), axis=0)
        if final >= 5:
            hop(5)

        normed = norm_call(ring.blocks, affine, slices)

        taps = tuple(range(3))
        units = [((0, taps), own), ((1, taps), pieces[1])]
        tokens = []

        def swapped(piece):
            return lax.ppermute(piece, "dp", ring.core_pairs)

        def arrived(i):
            units.append(((2 * i - 2, taps), pieces[i]))

        def swap(i):
            units.append(((2 * i - 1, taps), swapped(pieces[i])))

        windows = {}

        def convolve(total, count, extra=(), last=False, ahead=()):
            here = [units.pop(0) for _ in range(min(count, len(units)))]
            total, token, *made = conv_call(
                [p for p, _ in here], total, normed, [w for _, w in here], extra, last, windows, ahead
            )
            tokens.append(token)
            windows.update(zip(ahead, made))
            return total

        total = None
        for i in range(2, min(final, 3) + 1):
            arrived(i)
            swap(i)
        if final >= 4:
            total = convolve(total, 4)
        for i in range(6, final + 1):
            after = ([normed] + tokens)[i - 6]
            if i < final:
                hop(i, after)
            else:
                pieces[i - 2] = gate(pieces[i - 2], after)
                tail = [
                    (rows_of_taps, lax.ppermute(pieces[i - 2][rows_of_taps[0] : rows_of_taps[-1] + 1], "dp", ring.pairs))
                    for rows_of_taps in (taps[:2], taps[2:])
                ]
            arrived(i - 2)
            total = convolve(total, 4)
            swap(i - 2)
        if final >= 6:
            pieces[final - 1] = gate(pieces[final - 1], tokens[-1])
            arrived(final - 1)
        else:
            tail = []
            for i in range(4, final + 1):
                arrived(i)
                swap(i)
        while len(units) > 4:
            total = convolve(total, 4)
        extra = (skip[0], table)
        if tail:
            total = convolve(total, len(units), extra, ahead=(2 * final - 2, 2 * final - 1))
            extra = ()
            swap(final - 1)
        for rows_of_taps, piece in tail:
            piece = gate(piece, tokens[-1], times=1)
            if rows_of_taps == tail[0][0]:
                units.append(((2 * final - 2, rows_of_taps), piece))
            total = convolve(total, len(units))
            if rows_of_taps != tail[0][0]:
                units.append(((2 * final - 2, rows_of_taps), piece))
            units.append(((2 * final - 1, rows_of_taps), swapped(piece)))
        while len(units) > 2:
            total = convolve(total, min(4, len(units) - 2), extra)
            extra = ()
        total = convolve(total, len(units), extra, last=True)
        return total[None]

    return body


def solution(mesh):
    return jax.shard_map(
        make_body(mesh.shape["dp"], mesh.shape["chan"]),
        mesh=mesh,
        in_specs=(
            P("dp", "chan", None),
            P("dp", "chan", None),
            P("dp", None),
            P("dp", "chan"),
            P("chan"),
            P("chan"),
            P("chan"),
            P(None, "dp", "chan"),
            P("chan"),
        ),
        out_specs=P("dp", "chan", None),
        check_vma=False,
    )
```
